32 devices in a mesh: seq: 8 (over z, core), head: 4 (over y, x).
Axes of the slice: x: 2, y: 2, z: 4, core: 2. Of those that a mesh axis runs over, the one named last changes fastest.
Arguments:
- queries: bfloat16 [2048, 16, 128], P(('seq', 'head')), may hold values from -6 to 6
- keys: bfloat16 [2048, 16, 128], P(('seq', 'head')), may hold values from -6 to 6
- values: bfloat16 [2048, 16, 128], P(('seq', 'head')), may hold values from -6 to 6
- log_decay: bfloat16 [2048, 16], P(('seq', 'head')), may hold values from -1 to 0
- beta: bfloat16 [2048, 16], P(('seq', 'head')), may hold values from 0.0099 to 0.6
- norm_gain: float32 [128], replicated, may hold values from 0.25 to 1.75
Outputs:
- normed_core: bfloat16 [2048, 16, 128], P(('seq', 'head'))
The draws below stay inside these ranges and needn't reach their ends.
All inputs are finite; a program needn't handle non-finite values.
Results may differ from the reference program's by a relative error of at most 0.013.
Values may be sent and summed in bfloat16 or wider, within the bound.
A program may use at most 64 MiB of HBM per device.

```python
import jax
import jax.numpy as jnp
from jax import lax

H = 16
DK = 128
GROUP = 64
TOK_DEV = 64
DOCUMENT_TOKENS = 2048


def head_roles(key, quick_count):
    order = jax.random.permutation(jax.random.fold_in(key, 101), H)
    return order < quick_count


def draw_keys(key, part):
    sample_sequences = jax.random.split(jax.random.fold_in(key, 404), 2)
    shared = jax.random.normal(sample_sequences[0], (1, H, DK), jnp.float32)
    random_noise = jax.random.normal(sample_sequences[1], (DOCUMENT_TOKENS, H, DK), jnp.float32)
    strength = 0.8
    return jnp.clip(random_noise + strength * shared, -6.0, 6.0).astype(jnp.bfloat16)


def draw_log_decay(key, part):
    quick = head_roles(key, H // 2)
    sample_sequences = jax.random.split(jax.random.fold_in(key, 303), 6)
    slow_rate = jnp.exp(jax.random.uniform(sample_sequences[0], (H,), jnp.float32, jnp.log(0.05), jnp.log(0.5))) / DOCUMENT_TOKENS
    quick_rate = 1.0 / jax.random.uniform(sample_sequences[1], (H,), jnp.float32, 30.0, 50.0)
    decay_rates = jnp.where(quick, quick_rate, slow_rate)
    random_noise = jax.random.uniform(sample_sequences[2], (DOCUMENT_TOKENS, H), jnp.float32, 0.5, 2.0)
    blocks = jax.random.uniform(sample_sequences[3], (DOCUMENT_TOKENS // TOK_DEV, 1, H), jnp.float32, 0.5, 2.0)
    block_multiplier = jnp.broadcast_to(blocks, (DOCUMENT_TOKENS // TOK_DEV, TOK_DEV, H)).reshape(DOCUMENT_TOKENS, H)
    spike_probability = jax.random.uniform(sample_sequences[4], (DOCUMENT_TOKENS, 1), jnp.float32) < 3.0 / DOCUMENT_TOKENS
    spike_magnitude = jnp.log(jax.random.uniform(sample_sequences[5], (DOCUMENT_TOKENS, 1), jnp.float32, 0.5, 0.8))
    spike_events = jnp.where(spike_probability, spike_magnitude, 0.0)
    return (-decay_rates * random_noise * block_multiplier + spike_events).astype(jnp.bfloat16)


def draw_beta(key, part):
    quick = head_roles(key, H // 2)
    sample_sequences = jax.random.split(jax.random.fold_in(key, 202), 3)
    level = jnp.exp(jax.random.uniform(sample_sequences[0], (H,), jnp.float32, jnp.log(0.02), jnp.log(0.05)))
    random_noise = jax.random.uniform(sample_sequences[1], (DOCUMENT_TOKENS, H), jnp.float32, 0.5, 2.0)
    quick_beta = jax.random.uniform(sample_sequences[2], (DOCUMENT_TOKENS, H), jnp.float32, 0.05, 0.59)
    return jnp.where(quick, quick_beta, level * random_noise).astype(jnp.bfloat16)


def block_scale(key, dims, shards, low, top_value):
    factor_of, own = 1.0, jax.random.fold_in(key, 6)
    for axis_at, shards_of in shards:
        draws = jnp.exp(jax.random.uniform(jax.random.fold_in(own, axis_at), (shards_of,), jnp.float32, low / len(shards), top_value / len(shards)))
        factor_of = factor_of * jnp.repeat(draws, dims[axis_at] // shards_of).reshape([-1 if axis == axis_at else 1 for axis in range(len(dims))])
    return factor_of


def scatter_about(key, shape, scale, most, pieces=(), held_as=jnp.bfloat16):
    gain = block_scale(key, shape, pieces, -0.22, 0.18) if pieces else 1.0
    values = jax.random.normal(key, shape, jnp.float32) * scale * gain
    return jnp.minimum(jnp.maximum(values, -most), most).astype(held_as)


def setup_inputs(seed: int = 0) -> dict:
    seeds = jax.random.split(jax.random.key(seed), 7)
    queries = scatter_about(seeds[0], (DOCUMENT_TOKENS, H, DK), 1.0, 6.0, ((0, 32),))
    keys = draw_keys(jax.random.fold_in(seeds[6], 71), 0)
    values = scatter_about(seeds[2], (DOCUMENT_TOKENS, H, DK), 1.0, 6.0, ((0, 32),))
    log_decay = draw_log_decay(jax.random.fold_in(seeds[6], 71), 0)
    beta = draw_beta(jax.random.fold_in(seeds[6], 71), 0)
    norm_gain = jnp.clip(1.0 + 0.15 * jax.random.normal(seeds[5], (DK,), jnp.float32), 0.25, 1.75)
    return dict(queries=queries, keys=keys, values=values, log_decay=log_decay, beta=beta, norm_gain=norm_gain)


HIGH = lax.Precision.HIGHEST

def unit_rows(tensor):
    tensor = tensor.astype(jnp.float32)
    return tensor * lax.rsqrt(lax.optimization_barrier(jnp.sum(tensor * tensor, axis=-1, keepdims=True)) + 1e-06)

def key_terms(group_keys, group_values, group_gates, group_betas):
    cumulative = jnp.cumsum(group_gates, axis=-1)
    row_ids = lax.broadcasted_iota(jnp.int32, (GROUP, GROUP), 0)
    col_ids = lax.broadcasted_iota(jnp.int32, (GROUP, GROUP), 1)
    within = row_ids >= col_ids
    spread = jnp.where(within, jnp.exp(jnp.where(within, cumulative[..., :, None] - cumulative[..., None, :], 0.0)), 0.0)
    intersection = jnp.einsum('...id,...jd->...ij', group_keys, group_keys, precision=HIGH)
    lower_part = jnp.where(row_ids > col_ids, intersection * spread, 0.0) * group_betas[..., :, None]
    system = lower_part + jnp.eye(GROUP, dtype=jnp.float32)
    scaled = jnp.concatenate([group_values, group_keys * jnp.exp(cumulative)[..., None]], axis=-1) * group_betas[..., None]
    solved = jax.scipy.linalg.solve_triangular(system, scaled, lower=True, unit_diagonal=True)
    head_width = group_keys.shape[-1]
    pseudo = solved[..., :head_width]
    erasers = solved[..., head_width:]
    final_log = cumulative[..., -1:]
    carried = group_keys * jnp.exp(final_log - cumulative)[..., None]
    return (cumulative, spread, pseudo, erasers, carried, jnp.exp(final_log[..., 0]))

def reference(queries, keys, values, log_decay, beta, norm_gain):
    count = DOCUMENT_TOKENS // GROUP
    unit_q = (unit_rows(queries) * DK ** (-0.5)).astype(jnp.bfloat16)
    unit_k = unit_rows(keys).astype(jnp.bfloat16)

    def by_group(tensor):
        return tensor.astype(jnp.float32).reshape(count, GROUP, H, DK).transpose(0, 2, 1, 3)

    def gate_group(tensor):
        return tensor.astype(jnp.float32).reshape(count, GROUP, H).transpose(0, 2, 1)
    inputs_all = (by_group(unit_q), by_group(unit_k), by_group(values), gate_group(log_decay), gate_group(beta))

    def advance(state, inputs_one):
        group_q, group_k, group_v, group_g, group_b = inputs_one
        cumulative, spread, pseudo, erasers, carried, decays = key_terms(group_k, group_v, group_g, group_b)
        residue = pseudo - jnp.einsum('hcd,hde->hce', erasers, state, precision=HIGH)
        scores = jnp.einsum('hid,hjd->hij', group_q, group_k, precision=HIGH) * spread
        core = jnp.einsum('hcd,hde->hce', group_q * jnp.exp(cumulative)[..., None], state, precision=HIGH)
        core = core + jnp.einsum('hij,hje->hie', scores, residue, precision=HIGH)
        updated = decays[:, None, None] * state + jnp.einsum('hcd,hce->hde', carried, residue, precision=HIGH)
        return (updated, core)
    start = jnp.zeros((H, DK, DK), jnp.float32)
    _, cores = lax.scan(advance, start, inputs_all)
    core_rows = cores.transpose(0, 2, 1, 3).reshape(DOCUMENT_TOKENS, H, DK)
    scale_rows = lax.rsqrt(lax.optimization_barrier(jnp.mean(core_rows * core_rows, axis=-1, keepdims=True)) + 1e-06)
    return (core_rows * scale_rows * norm_gain).astype(jnp.bfloat16)
```

```python
import functools

import jax
import jax.numpy as jnp
from jax import lax
from jax.experimental import pallas as pl
from jax.experimental.pallas import tpu as pltpu
from jax.sharding import PartitionSpec as P

PACK = 4
MESH = pl.DeviceIdType.MESH
F32, BF16 = jnp.float32, jnp.bfloat16


def dot(left, right, dims=((1,), (0,))):
    return lax.dot_general(left, right, (dims, ((), ())), preferred_element_type=F32)


def split(tensor):
    high = tensor.astype(BF16)
    return high, (tensor - high.astype(F32)).astype(BF16)


def dot3(left, right):
    left_high, left_low = split(left)
    right_high, right_low = split(right)
    return dot(left_high, right_high) + (dot(left_low, right_high) + dot(left_high, right_low))


def unit(tensor):
    flat = tensor.astype(F32).reshape(-1, tensor.shape[-1])
    return flat * lax.rsqrt(jnp.sum(flat * flat, axis=-1, keepdims=True) + 1e-06)


def kernel(
    n_seq, n_head, q_ref, k_ref, v_ref, decay_ref, beta_ref, gain_ref, out_ref,
    q_rows, k_rows, v_rows, out_rows, terms_out, terms_in, through, offset,
    maps_high, maps_low, maps_add, chain_in, chain_out, states_out, states_in,
    terms_send, terms_recv, chain_send, chain_recv, states_send, states_recv,
):
    seq, me = lax.axis_index("seq"), lax.axis_index("head")
    tokens, heads, width = q_ref.shape
    own = heads // n_head
    rows = own * tokens

    def partner(step):
        return {"head": lax.rem(me + step, n_head)}

    barrier = pltpu.get_barrier_semaphore()
    for step in range(1, n_head):
        pl.semaphore_signal(barrier, inc=1, device_id=partner(step), device_id_type=MESH)
    for side in (1, n_seq - 1):
        pl.semaphore_signal(
            barrier, inc=1, device_id={"seq": lax.rem(seq + side, n_seq)}, device_id_type=MESH
        )

    k_rows[...] = unit(k_ref[...])
    v_rows[...] = v_ref[...].astype(F32).reshape(-1, width)
    q_rows[...] = unit(q_ref[...]) * width ** (-0.5)

    row_t = lax.broadcasted_iota(jnp.int32, (tokens, tokens), 0)
    col_t = lax.broadcasted_iota(jnp.int32, (tokens, tokens), 1)
    cumulative = dot(jnp.where(row_t >= col_t, 1.0, 0.0).astype(BF16), decay_ref[...])
    betas = beta_ref[...].astype(F32)
    lane = lax.broadcasted_iota(jnp.int32, (tokens, heads), 1)

    size = PACK * tokens
    row = lax.broadcasted_iota(jnp.int32, (size, size), 0)
    col = lax.broadcasted_iota(jnp.int32, (size, size), 1)

    def same(block):
        return (row // block) == (col // block)

    within = same(tokens) & (row >= col)
    strict = same(tokens) & (row > col)
    identity = jnp.where(row == col, 1.0, 0.0)

    def terms_copy(step):
        return pltpu.make_async_remote_copy(
            src_ref=terms_out.at[step], dst_ref=terms_in.at[me],
            send_sem=terms_send.at[step], recv_sem=terms_recv.at[step],
            device_id=partner(step), device_id_type=MESH,
        )

    def pack_terms(units):
        ids = [lax.rem(me + step, n_head) * own + part for step, part in units]

        def stack(ref):
            return jnp.concatenate([ref[pl.ds(i, tokens, stride=heads), :] for i in ids], axis=0)

        def column(gate, i):
            picked = jnp.sum(jnp.where(lane == i, gate, 0.0), axis=1, keepdims=True)
            return jnp.broadcast_to(picked, (tokens, width))

        cums = [column(cumulative, i) for i in ids]
        ends = [jnp.broadcast_to(c[tokens - 1 :, :], (tokens, width)) for c in cums]
        cum = jnp.concatenate(cums, axis=0)
        end = jnp.concatenate(ends, axis=0)
        beta = jnp.concatenate([column(betas, i) for i in ids], axis=0)
        wide = lambda t: jnp.concatenate([t] * (size // width), axis=1)
        across = jnp.transpose(cum)[0:1, :]
        spread = jnp.exp(jnp.where(within, wide(cum) - across, -1e30))
        keys = stack(k_rows).astype(BF16)
        keys_wide = keys.astype(F32)
        lower = jnp.where(strict, dot(keys, keys, ((1,), (1,))) * spread, 0.0) * wide(beta)
        power = jnp.where(same(16), lower, 0.0)
        inverse = identity - power
        for _ in range(3):
            power = dot3(power, power)
            inverse = inverse + dot3(inverse, power)
        block = 16
        while block < tokens:
            corner = jnp.where(same(2 * block) & ~same(block), lower, 0.0)
            inverse = inverse - dot3(dot3(inverse, corner), inverse)
            block *= 2
        grown = jnp.exp(cum)
        right = jnp.concatenate([stack(v_rows) * beta, keys_wide * (grown * beta)], axis=1)
        solved = dot3(inverse, right)
        pseudo, erasers = solved[:, :width].astype(BF16), solved[:, width:].astype(BF16)
        carried = (keys_wide * jnp.exp(end - cum)).astype(BF16)
        decays = [jnp.exp(c[tokens - 1 :, :]) for c in cums]
        return ids, cum, spread, keys, pseudo, erasers, carried, decays, grown

    def store_terms(units, data):
        _, _, _, _, pseudo, erasers, carried, decays, _ = data
        tail_row = lax.broadcasted_iota(jnp.int32, (16, width), 0)
        for at in range(0, PACK, own):
            step = units[at][0]
            tail = jnp.zeros((16, width), F32)
            for part in range(own):
                high, low = split(decays[at + part])
                tail = jnp.where(tail_row == 2 * part, high.astype(F32), tail)
                tail = jnp.where(tail_row == 2 * part + 1, low.astype(F32), tail)
            section = slice(at * tokens, at * tokens + rows)
            target = terms_in.at[me] if step == 0 else terms_out.at[step]
            target[0:rows, :] = pseudo[section]
            target[rows : 2 * rows, :] = erasers[section]
            target[2 * rows : 3 * rows, :] = carried[section]
            target[3 * rows :, :] = tail.astype(BF16)
            if step:
                terms_copy(step).start()

    def query_terms(base, data):
        ids, _, spread, keys, pseudo, erasers, _, _, grown = data
        queries = jnp.concatenate(
            [q_rows[pl.ds(i, tokens, stride=heads), :] for i in ids], axis=0
        ).astype(BF16)
        scores = (dot(queries, keys, ((1,), (1,))) * spread).astype(BF16)
        mixed = dot(scores, jnp.concatenate([pseudo, erasers], axis=1))
        through[base : base + size, :] = (
            queries.astype(F32) * grown - mixed[:, width:]
        ).astype(BF16)
        offset[base : base + size, :] = mixed[:, :width]

    order = list(range(1, n_head)) + [0]
    units = [(step, part) for step in order for part in range(own)]
    packs = [units[at : at + PACK] for at in range(0, len(units), PACK)]
    kept = []
    for at, pack in enumerate(packs):
        data = pack_terms(pack)
        if at == 0:
            pl.semaphore_wait(barrier, n_head + 1)
        store_terms(pack, data)
        kept.append(data)
    for at, data in enumerate(kept):
        query_terms(at * size, data)

    for step in range(1, n_head):
        terms_copy(step).wait_recv()
    eye = jnp.where(
        lax.broadcasted_iota(jnp.int32, (width, width), 0)
        == lax.broadcasted_iota(jnp.int32, (width, width), 1), 1.0, 0.0,
    )
    for part in range(own):
        current = jnp.concatenate([eye, jnp.zeros((width, width), F32)], axis=1)
        for group in range(n_head + 1):
            high, low = split(current[:, :width])
            section = slice(group * width, (group + 1) * width)
            maps_high[part, section, :] = high
            maps_low[part, section, :] = low
            maps_add[part, section, :] = current[:, width:]
            if group == n_head:
                break
            at = part * tokens
            pseudo = terms_in[group, at : at + tokens, :]
            erasers = terms_in[group, rows + at : rows + at + tokens, :]
            carried = terms_in[group, 2 * rows + at : 2 * rows + at + tokens, :]
            tail = terms_in[group, 3 * rows :, :].astype(F32)
            decay = tail[2 * part : 2 * part + 1, :] + tail[2 * part + 1 : 2 * part + 2, :]
            erased = dot(erasers, current.astype(BF16))
            change = jnp.concatenate(
                [erased[:, :width], erased[:, width:] - pseudo.astype(F32)], axis=1
            ).astype(BF16)
            current = current * jnp.concatenate([decay, decay], axis=1) - dot(
                carried, change, ((0,), (0,))
            )

    def chain_copy(part):
        return pltpu.make_async_remote_copy(
            src_ref=chain_out.at[part], dst_ref=chain_in.at[part],
            send_sem=chain_send.at[part], recv_sem=chain_recv.at[part],
            device_id={"seq": lax.rem(seq + 1, n_seq)}, device_id_type=MESH,
        )

    def states_copy(step, part):
        slot = n_head - step
        return pltpu.make_async_remote_copy(
            src_ref=states_out.at[step, part], dst_ref=states_in.at[slot, part],
            send_sem=states_send.at[step, part], recv_sem=states_recv.at[slot, part],
            device_id=partner(step), device_id_type=MESH,
        )

    def mapped(part, group, state):
        section = pl.ds(pl.multiple_of(group * width, width), width)
        high, low = state
        first = maps_high[part, section, :]
        return (
            dot(first, high) + (dot(maps_low[part, section, :], high) + dot(first, low))
        ) + maps_add[part, section, :]

    @pl.when(seq == 0)
    def _():
        chain_in[...] = jnp.zeros_like(chain_in)

    def give_states(part):
        state = split(chain_in[part])
        for step in order:
            entry = mapped(part, lax.rem(me + step, n_head), state).astype(BF16)
            if step:
                states_out[step, part] = entry
                states_copy(step, part).start()
            else:
                states_in[0, part] = entry

    for part in range(own):
        @pl.when(seq > 0)
        def _():
            chain_copy(part).wait_recv()

        chain_out[part] = mapped(part, n_head, split(chain_in[part]))

        @pl.when(seq < n_seq - 1)
        def _():
            chain_copy(part).start()

        if part:
            give_states(part - 1)
    give_states(own - 1)

    gain = gain_ref[...]
    for step in [0] + list(range(n_head - 1, 0, -1)):
        for part in range(own):
            if step:
                states_copy(n_head - step, part).wait_recv()
            at = (order.index(step) * own + part) * tokens
            core = dot(through[at : at + tokens, :], states_in[step, part])
            core = core + offset[at : at + tokens, :]
            scale = lax.rsqrt(jnp.mean(core * core, axis=-1, keepdims=True) + 1e-06)
            head = lax.rem(me + step, n_head) * own + part
            out_rows[pl.ds(head, tokens, stride=heads), :] = core * scale * gain
    out_ref[...] = out_rows[...].reshape(tokens, heads, width).astype(BF16)

    for step in range(1, n_head):
        terms_copy(step).wait_send()
        for part in range(own):
            states_copy(step, part).wait_send()

    @pl.when(seq < n_seq - 1)
    def _():
        for part in range(own):
            chain_copy(part).wait_send()


def solution(mesh):
    n_seq, n_head = mesh.shape["seq"], mesh.shape["head"]

    def local(queries, keys, values, log_decay, beta, norm_gain):
        tokens, heads, width = queries.shape
        own = heads // n_head
        length = tokens * heads
        vmem = pl.BlockSpec(memory_space=pltpu.VMEM)
        payload = (n_head, 3 * own * tokens + 16, width)
        maps = (own, (n_head + 1) * width, width)
        dma = pltpu.SemaphoreType.DMA
        return pl.pallas_call(
            functools.partial(kernel, n_seq, n_head),
            out_shape=jax.ShapeDtypeStruct(queries.shape, BF16),
            in_specs=[vmem] * 6,
            out_specs=vmem,
            scratch_shapes=[
                pltpu.VMEM((length, width), F32),
                pltpu.VMEM((length, width), F32),
                pltpu.VMEM((length, width), F32),
                pltpu.VMEM((length, width), F32),
                pltpu.VMEM(payload, BF16),
                pltpu.VMEM(payload, BF16),
                pltpu.VMEM((length, width), BF16),
                pltpu.VMEM((length, width), F32),
                pltpu.VMEM(maps, BF16),
                pltpu.VMEM(maps, BF16),
                pltpu.VMEM(maps, F32),
                pltpu.VMEM((own, width, width), F32),
                pltpu.VMEM((own, width, width), F32),
                pltpu.VMEM((n_head, own, width, width), BF16),
                pltpu.VMEM((n_head, own, width, width), BF16),
                dma((n_head,)),
                dma((n_head,)),
                dma((own,)),
                dma((own,)),
                dma((n_head, own)),
                dma((n_head, own)),
            ],
            compiler_params=pltpu.CompilerParams(
                collective_id=0, has_side_effects=True, vmem_limit_bytes=48 * 1024 * 1024
            ),
            name="gated_delta",
        )(queries, keys, values, log_decay, beta, norm_gain.reshape(1, width))

    tokens_by_device = P(("seq", "head"), None, None)
    placed = (tokens_by_device,) * 3 + (P(("seq", "head"), None),) * 2 + (P(),)
    return jax.shard_map(
        local, mesh=mesh, in_specs=placed, out_specs=tokens_by_device, check_vma=False
    )
```

```python
import functools

import jax
import jax.numpy as jnp
from jax import lax
from jax.experimental import pallas as pl
from jax.experimental.pallas import tpu as pltpu
from jax.sharding import PartitionSpec as P

PACK = 2
BATCH = 4
MESH = pl.DeviceIdType.MESH
F32, BF16 = jnp.float32, jnp.bfloat16
NT, TN = ((1,), (1,)), ((0,), (0,))


def dot(left, right, dims=((1,), (0,))):
    return lax.dot_general(left, right, (dims, ((), ())), preferred_element_type=F32)


def short(tensors):
    return [tensor.astype(BF16) for tensor in tensors]


def unit(tensor):
    flat = tensor.astype(F32).reshape(-1, tensor.shape[-1])
    return flat * lax.rsqrt(jnp.sum(flat * flat, axis=-1, keepdims=True) + 1e-06)


def kernel(
    n_seq, n_head, q_hbm, k_hbm, v_hbm, decay_hbm, beta_hbm, gain_hbm, out_ref,
    q_ref, k_ref, v_ref, decay_ref, beta_ref, gain_ref,
    q_rows, k_rows, v_rows, row_gate, terms_out, terms_in, query_out, query_in, offset,
    prefix, slab_high, slab_low, slab_add, query_map, query_add,
    chain_in, chain_out, core_out, core_in,
    load_sem, terms_send, terms_recv, query_send, query_recv,
    chain_send, chain_recv, core_send, core_recv,
):
    seq, me = lax.axis_index("seq"), lax.axis_index("head")
    tokens, heads, width = q_ref.shape
    own = heads // n_head
    rows = own * tokens

    def partner(step):
        return {"head": lax.rem(me + step, n_head)}

    sources = (decay_hbm, beta_hbm, k_hbm, v_hbm, q_hbm, gain_hbm)
    targets = (decay_ref, beta_ref, k_ref, v_ref, q_ref, gain_ref)
    loads = [
        pltpu.make_async_copy(source, target, load_sem.at[at])
        for at, (source, target) in enumerate(zip(sources, targets))
    ]
    for load in loads:
        load.start()

    barrier = pltpu.get_barrier_semaphore()
    for step in range(1, n_head):
        pl.semaphore_signal(barrier, inc=1, device_id=partner(step), device_id_type=MESH)
    for side in (1, n_seq - 1):
        pl.semaphore_signal(
            barrier, inc=1, device_id={"seq": lax.rem(seq + side, n_seq)}, device_id_type=MESH
        )

    size = PACK * tokens
    row = lax.broadcasted_iota(jnp.int32, (size, size), 0)
    col = lax.broadcasted_iota(jnp.int32, (size, size), 1)

    def same(block):
        return (row // block) == (col // block)

    within = same(tokens) & (row >= col)
    strict = same(tokens) & (row > col)
    identity = jnp.where(row == col, 1.0, 0.0)
    first_head = lax.broadcasted_iota(jnp.int32, (1, size), 1) < tokens
    row_t = lax.broadcasted_iota(jnp.int32, (tokens, tokens), 0)
    col_t = lax.broadcasted_iota(jnp.int32, (tokens, tokens), 1)
    token_of = lax.rem(lax.broadcasted_iota(jnp.int32, (tokens, size), 1), tokens)
    before = lax.broadcasted_iota(jnp.int32, (tokens, size), 0) <= token_of
    lane = lax.broadcasted_iota(jnp.int32, (tokens, heads), 1)

    loads[0].wait()
    row_gate[...] = dot(decay_ref[...], jnp.where(before, 1.0, 0.0).astype(BF16))
    cumulative = dot(jnp.where(row_t >= col_t, 1.0, 0.0).astype(BF16), decay_ref[...], NT)
    loads[1].wait()
    betas = dot(jnp.where(row_t == col_t, 1.0, 0.0).astype(BF16), beta_ref[...], NT)
    loads[2].wait()
    k_rows[...] = unit(k_ref[...])
    loads[3].wait()
    v_rows[...] = v_ref[...].astype(F32).reshape(-1, width)
    loads[4].wait()
    q_rows[...] = unit(q_ref[...]) * width ** (-0.5)
    loads[5].wait()

    def stack(ref, ids):
        return jnp.concatenate([ref[pl.ds(i, tokens, stride=heads), :] for i in ids], axis=0)

    def column(gate, i):
        picked = jnp.sum(jnp.where(lane == i, gate, 0.0), axis=1, keepdims=True)
        return jnp.broadcast_to(picked, (tokens, width))

    def batch_terms(packs):
        ids = [[lax.rem(me + step, n_head) * own + part for step, part in pack] for pack in packs]
        cums = [[column(cumulative, i) for i in pack] for pack in ids]
        ends = [[c[tokens - 1 :, :] for c in pack] for pack in cums]
        cum = [jnp.concatenate(pack, axis=0) for pack in cums]
        end = [
            jnp.concatenate([jnp.broadcast_to(e, (tokens, width)) for e in pack], axis=0)
            for pack in ends
        ]
        beta = [jnp.concatenate([column(betas, i) for i in pack], axis=0) for pack in ids]
        across = [
            jnp.where(first_head, row_gate[pl.ds(pack[0], 1), :], row_gate[pl.ds(pack[1], 1), :])
            for pack in ids
        ]
        spread = [jnp.exp(jnp.where(within, c - a, -1e30)) for c, a in zip(cum, across)]
        keys = [stack(k_rows, pack).astype(BF16) for pack in ids]
        lower = [
            jnp.where(strict, dot(k, k, NT) * s, 0.0) * b for k, s, b in zip(keys, spread, beta)
        ]
        block = 8
        inner = [jnp.where(same(block), a, 0.0) for a in lower]
        inner_short = short(inner)
        inverse = [identity - a for a in inner]
        square = short([dot(a, a) for a in inner_short])
        fourth = short([dot(a, a) for a in square])
        inverse = [x + dot(y, a) for x, y, a in zip(inverse, short(inverse), square)]
        inverse = [x + dot(y, a) for x, y, a in zip(inverse, short(inverse), fourth)]
        grown = [jnp.exp(c) for c in cum]
        wide = [k.astype(F32) for k in keys]
        right = short([
            jnp.concatenate([stack(v_rows, pack) * b, w * (g * b)], axis=1)
            for pack, b, w, g in zip(ids, beta, wide, grown)
        ])
        while block < tokens:
            between = same(2 * block) & ~same(block)
            corner = short([jnp.where(between, a, 0.0) for a in lower])
            held = short(inverse)
            crossed = short([dot(x, a) for x, a in zip(held, corner)])
            block *= 2
            if block < tokens:
                inverse = [x - dot(a, y) for x, a, y in zip(inverse, crossed, held)]
        partly = [dot(x, r) for x, r in zip(held, right)]
        solved = short([y - dot(a, z) for y, a, z in zip(partly, crossed, short(partly))])
        carried = short([w * jnp.exp(e - c) for w, e, c in zip(wide, end, cum)])
        decays = [[jnp.exp(e) for e in pack] for pack in ends]
        return [
            dict(units=pack, ids=i, spread=s, keys=k, solved=x, carried=c, decays=d, grown=g)
            for pack, i, s, k, x, c, d, g in zip(
                packs, ids, spread, keys, solved, carried, decays, grown
            )
        ]

    def terms_copy(step):
        return pltpu.make_async_remote_copy(
            src_ref=terms_out.at[step], dst_ref=terms_in.at[me],
            send_sem=terms_send.at[step], recv_sem=terms_recv.at[step],
            device_id=partner(step), device_id_type=MESH,
        )

    def query_copy(step):
        return pltpu.make_async_remote_copy(
            src_ref=query_out.at[step], dst_ref=query_in.at[me],
            send_sem=query_send.at[step], recv_sem=query_recv.at[step],
            device_id=partner(step), device_id_type=MESH,
        )

    tail_row = lax.broadcasted_iota(jnp.int32, (16, width), 0)

    def store_terms(batch):
        by_step = {}
        for data in batch:
            for at, (step, part) in enumerate(data["units"]):
                target = terms_in.at[me] if step == 0 else terms_out.at[step]
                section, to = slice(at * tokens, (at + 1) * tokens), part * tokens
                target[to : to + tokens, :] = data["solved"][section, :width]
                target[rows + to : rows + to + tokens, :] = data["solved"][section, width:]
                target[2 * rows + to : 2 * rows + to + tokens, :] = data["carried"][section]
                tail = by_step.get(step, jnp.zeros((16, width), F32))
                decay = data["decays"][at]
                high = decay.astype(BF16).astype(F32)
                tail = jnp.where(tail_row == 2 * part, high, tail)
                by_step[step] = jnp.where(tail_row == 2 * part + 1, decay - high, tail)
        for step, tail in by_step.items():
            target = terms_in.at[me] if step == 0 else terms_out.at[step]
            target[3 * rows :, :] = tail.astype(BF16)
            if step:
                terms_copy(step).start()

    def query_terms(batch):
        queries = [stack(q_rows, data["ids"]).astype(BF16) for data in batch]
        scores = short([dot(q, d["keys"], NT) * d["spread"] for q, d in zip(queries, batch)])
        mixed = [dot(s, d["solved"]) for s, d in zip(scores, batch)]
        for q, m, d in zip(queries, mixed, batch):
            through = (q.astype(F32) * d["grown"] - m[:, width:]).astype(BF16)
            for at, (step, part) in enumerate(d["units"]):
                section, to = slice(at * tokens, (at + 1) * tokens), part * tokens
                target = query_in.at[me] if step == 0 else query_out.at[step]
                target[to : to + tokens, :] = through[section]
                offset[step, part] = m[section, :width]

    order = list(range(1, n_head)) + [0]
    units = [(step, part) for step in order for part in range(own)]
    packs = [units[at : at + PACK] for at in range(0, len(units), PACK)]
    kept = []
    for at in range(0, len(packs), BATCH):
        batch = batch_terms(packs[at : at + BATCH])
        if at == 0:
            pl.semaphore_wait(barrier, n_head + 1)
        store_terms(batch)
        kept.append(batch)
    for batch in kept:
        query_terms(batch)
    for step in range(1, n_head):
        query_copy(step).start()

    for step in range(1, n_head):
        terms_copy(step).wait_recv()
    eye = jnp.where(
        lax.broadcasted_iota(jnp.int32, (width, width), 0)
        == lax.broadcasted_iota(jnp.int32, (width, width), 1), 1.0, 0.0,
    )
    current = [jnp.concatenate([eye, jnp.zeros((width, width), F32)], axis=1)] * own
    for group in range(n_head):
        tail = terms_in[group, 3 * rows :, :].astype(F32)
        held = short(current)
        for part in range(own):
            prefix[part, group] = held[part]
        for part in range(own):
            at = part * tokens
            pseudo = terms_in[group, at : at + tokens, :]
            erasers = terms_in[group, rows + at : rows + at + tokens, :]
            carried = terms_in[group, 2 * rows + at : 2 * rows + at + tokens, :]
            decay = tail[2 * part : 2 * part + 1, :] + tail[2 * part + 1 : 2 * part + 2, :]
            if group:
                erased = dot(erasers, held[part])
                change = jnp.concatenate(
                    [erased[:, :width], erased[:, width:] - pseudo.astype(F32)], axis=1
                ).astype(BF16)
            else:
                change = jnp.concatenate([erasers, -pseudo], axis=1)
            decay = jnp.concatenate([decay, decay], axis=1)
            current[part] = current[part] * decay - dot(carried, change, TN)
    for part in range(own):
        high = current[part][:, :width].astype(BF16)
        slab_high[part] = high
        slab_low[part] = (current[part][:, :width] - high.astype(F32)).astype(BF16)
        slab_add[part] = current[part][:, width:]

    def chain_copy(part):
        return pltpu.make_async_remote_copy(
            src_ref=chain_out.at[part], dst_ref=chain_in.at[part],
            send_sem=chain_send.at[part], recv_sem=chain_recv.at[part],
            device_id={"seq": lax.rem(seq + 1, n_seq)}, device_id_type=MESH,
        )

    def core_copy(step, part):
        slot = n_head - step
        group = lax.rem(me + step, n_head)
        return pltpu.make_async_remote_copy(
            src_ref=core_out.at[part, group], dst_ref=core_in.at[slot, part],
            send_sem=core_send.at[step, part], recv_sem=core_recv.at[slot, part],
            device_id=partner(step), device_id_type=MESH,
        )

    def map_queries():
        for step in range(1, n_head):
            query_copy(step).wait_recv()
        for group in range(n_head):
            for part in range(own):
                section = slice(group * tokens, (group + 1) * tokens)
                at = part * tokens
                queries = query_in[group, at : at + tokens, :]
                mapped = dot(queries, prefix[part, group])
                query_map[part, section, :] = mapped[:, :width].astype(BF16)
                query_add[part, section, :] = mapped[:, width:]

    def pass_on(part):
        @pl.when(seq > 0)
        def _():
            chain_copy(part).wait_recv()

        @pl.when(seq < n_seq - 1)
        def _():
            state = chain_in[part]
            moved = dot(slab_high[part], state) + dot(slab_low[part], state)
            chain_out[part] = (moved + slab_add[part]).astype(BF16)
            chain_copy(part).start()

    def give_cores(part):
        cores = dot(query_map[part], chain_in[part]) + query_add[part]
        core_out[part] = cores.astype(BF16).reshape(n_head, tokens, width)
        for step in range(1, n_head):
            core_copy(step, part).start()

    @pl.when(seq == 0)
    def _():
        chain_in[...] = jnp.zeros_like(chain_in)

    late = seq >= n_seq // 2

    @pl.when(late)
    def _():
        map_queries()
        for part in range(own):
            pass_on(part)
            give_cores(part)

    @pl.when(jnp.logical_not(late))
    def _():
        for part in range(own):
            pass_on(part)
        map_queries()
        for part in range(own):
            give_cores(part)

    gain = gain_ref[...]
    for step in [0] + list(range(n_head - 1, 0, -1)):
        for part in range(own):
            if step:
                core_copy(n_head - step, part).wait_recv()
                core = core_in[step, part]
            else:
                core = core_out[part, me]
            core = core.astype(F32) + offset[step, part]
            scale = lax.rsqrt(jnp.mean(core * core, axis=-1, keepdims=True) + 1e-06)
            head = lax.rem(me + step, n_head) * own + part
            out_ref[pl.ds(head, tokens, stride=heads), :] = core * scale * gain

    for step in range(1, n_head):
        terms_copy(step).wait_send()
        query_copy(step).wait_send()
        for part in range(own):
            core_copy(step, part).wait_send()

    @pl.when(seq < n_seq - 1)
    def _():
        for part in range(own):
            chain_copy(part).wait_send()


def solution(mesh):
    n_seq, n_head = mesh.shape["seq"], mesh.shape["head"]

    def local(queries, keys, values, log_decay, beta, norm_gain):
        tokens, heads, width = queries.shape
        own = heads // n_head
        length = tokens * heads
        hbm = pl.BlockSpec(memory_space=pltpu.HBM)
        payload = (n_head, 3 * own * tokens + 16, width)
        dma = pltpu.SemaphoreType.DMA
        rows = pl.pallas_call(
            functools.partial(kernel, n_seq, n_head),
            out_shape=jax.ShapeDtypeStruct((length, width), F32),
            in_specs=[hbm] * 6,
            out_specs=pl.BlockSpec(memory_space=pltpu.VMEM),
            scratch_shapes=[
                pltpu.VMEM(queries.shape, BF16),
                pltpu.VMEM(queries.shape, BF16),
                pltpu.VMEM(queries.shape, BF16),
                pltpu.VMEM((heads, tokens), BF16),
                pltpu.VMEM((heads, tokens), BF16),
                pltpu.VMEM((1, width), F32),
                pltpu.VMEM((length, width), F32),
                pltpu.VMEM((length, width), F32),
                pltpu.VMEM((length, width), F32),
                pltpu.VMEM((heads, PACK * tokens), F32),
                pltpu.VMEM(payload, BF16),
                pltpu.VMEM(payload, BF16),
                pltpu.VMEM((n_head, own * tokens, width), BF16),
                pltpu.VMEM((n_head, own * tokens, width), BF16),
                pltpu.VMEM((n_head, own, tokens, width), F32),
                pltpu.VMEM((own, n_head, width, 2 * width), BF16),
                pltpu.VMEM((own, width, width), BF16),
                pltpu.VMEM((own, width, width), BF16),
                pltpu.VMEM((own, width, width), F32),
                pltpu.VMEM((own, n_head * tokens, width), BF16),
                pltpu.VMEM((own, n_head * tokens, width), F32),
                pltpu.VMEM((own, width, width), BF16),
                pltpu.VMEM((own, width, width), BF16),
                pltpu.VMEM((own, n_head, tokens, width), BF16),
                pltpu.VMEM((n_head, own, tokens, width), BF16),
                dma((6,)),
                dma((n_head,)),
                dma((n_head,)),
                dma((n_head,)),
                dma((n_head,)),
                dma((own,)),
                dma((own,)),
                dma((n_head, own)),
                dma((n_head, own)),
            ],
            compiler_params=pltpu.CompilerParams(
                collective_id=0, has_side_effects=True, vmem_limit_bytes=63 * 1024 * 1024
            ),
            name="gated_delta",
        )(queries, keys, values, log_decay.T, beta.T, norm_gain.reshape(1, width))
        return rows.reshape(tokens, heads, width).astype(BF16)

    tokens_by_device = P(("seq", "head"), None, None)
    placed = (tokens_by_device,) * 3 + (P(("seq", "head"), None),) * 2 + (P(),)
    return jax.shard_map(
        local, mesh=mesh, in_specs=placed, out_specs=tokens_by_device, check_vma=False
    )
```

```python
import functools

import jax
import jax.numpy as jnp
from jax import lax
from jax.experimental import pallas as pl
from jax.experimental.pallas import tpu as pltpu
from jax.sharding import PartitionSpec as P

PACK = 2
BATCH = 8
MESH = pl.DeviceIdType.MESH
F32, BF16 = jnp.float32, jnp.bfloat16
NT, TN = ((1,), (1,)), ((0,), (0,))


def dot(left, right, dims=((1,), (0,))):
    return lax.dot_general(left, right, (dims, ((), ())), preferred_element_type=F32)


def short(tensors):
    return [tensor.astype(BF16) for tensor in tensors]


def unit(tensor):
    flat = tensor.astype(F32).reshape(-1, tensor.shape[-1])
    return flat * lax.rsqrt(jnp.sum(flat * flat, axis=-1, keepdims=True) + 1e-06)


def kernel(
    n_seq, n_head, q_hbm, k_hbm, v_hbm, decay_hbm, beta_hbm, gain_hbm, out_ref,
    q_ref, k_ref, v_ref, decay_ref, beta_ref, gain_ref,
    q_rows, k_rows, v_rows, out_rows, row_gate, beta_rows, kept_gate, terms_out, terms_in, solver_out, solver_in, query_out, query_in, offset,
    prefix, slab_high, slab_low, slab_add, query_map, query_add,
    chain_in, chain_out, core_out, core_in,
    load_sem, terms_send, terms_recv, solver_send, solver_recv, query_send, query_recv,
    chain_send, chain_recv, core_send, core_recv,
):
    seq, me = lax.axis_index("seq"), lax.axis_index("head")
    tokens, heads, width = q_ref.shape
    own = heads // n_head
    rows = own * tokens

    def partner(step):
        return {"head": lax.rem(me + step, n_head)}

    sources = (decay_hbm, beta_hbm, k_hbm, v_hbm, q_hbm, gain_hbm)
    targets = (decay_ref, beta_ref, k_ref, v_ref, q_ref, gain_ref)
    loads = [
        pltpu.make_async_copy(source, target, load_sem.at[at])
        for at, (source, target) in enumerate(zip(sources, targets))
    ]
    for load in loads:
        load.start()

    barrier = pltpu.get_barrier_semaphore()
    for step in range(1, n_head):
        pl.semaphore_signal(barrier, inc=1, device_id=partner(step), device_id_type=MESH)
    for side in (1, n_seq - 1):
        pl.semaphore_signal(
            barrier, inc=1, device_id={"seq": lax.rem(seq + side, n_seq)}, device_id_type=MESH
        )

    size = PACK * tokens
    row = lax.broadcasted_iota(jnp.int32, (size, size), 0)
    col = lax.broadcasted_iota(jnp.int32, (size, size), 1)

    def same(block):
        return (row // block) == (col // block)

    within = same(tokens) & (row >= col)
    strict = same(tokens) & (row > col)
    identity = jnp.where(row == col, 1.0, 0.0)
    first_head = lax.broadcasted_iota(jnp.int32, (1, size), 1) < tokens
    row_t = lax.broadcasted_iota(jnp.int32, (tokens, tokens), 0)
    col_t = lax.broadcasted_iota(jnp.int32, (tokens, tokens), 1)
    token_of = lax.rem(lax.broadcasted_iota(jnp.int32, (tokens, size), 1), tokens)
    before = lax.broadcasted_iota(jnp.int32, (tokens, size), 0) <= token_of
    lane = lax.broadcasted_iota(jnp.int32, (tokens, heads), 1)

    loads[0].wait()
    log_rows = dot(decay_ref[...], jnp.where(before, 1.0, 0.0).astype(BF16))
    row_gate[...] = log_rows
    log_end = log_rows[:, size - 1 :]
    first_half = lax.broadcasted_iota(jnp.int32, (heads, size), 1) < tokens
    kept_gate[0] = jnp.exp(jnp.where(first_half, log_rows, log_end - log_rows))
    kept_gate[1] = jnp.broadcast_to(jnp.exp(log_end), (heads, size))
    cumulative = dot(jnp.where(row_t >= col_t, 1.0, 0.0).astype(BF16), decay_ref[...], NT)
    loads[1].wait()
    row_beta = dot(beta_ref[...], jnp.where(token_of == lax.broadcasted_iota(
        jnp.int32, (tokens, size), 0), 1.0, 0.0).astype(BF16))
    beta_rows[...] = row_beta
    betas = dot(jnp.where(row_t == col_t, 1.0, 0.0).astype(BF16), beta_ref[...], NT)
    loads[2].wait()
    k_rows[...] = unit(k_ref[...])
    loads[3].wait()
    v_rows[...] = v_ref[...].astype(F32).reshape(-1, width)
    def stack(ref, ids):
        return jnp.concatenate([ref[pl.ds(i, tokens, stride=heads), :] for i in ids], axis=0)

    def column(gate, i):
        picked = jnp.sum(jnp.where(lane == i, gate, 0.0), axis=1, keepdims=True)
        return jnp.broadcast_to(picked, (tokens, width))

    def batch_terms(packs):
        ids = [[lax.rem(me + step, n_head) * own + part for step, part in pack] for pack in packs]
        cums = [[column(cumulative, i) for i in pack] for pack in ids]
        cum = [jnp.concatenate(pack, axis=0) for pack in cums]
        beta = [jnp.concatenate([column(betas, i) for i in pack], axis=0) for pack in ids]
        across = [
            jnp.where(first_head, row_gate[pl.ds(pack[0], 1), :], row_gate[pl.ds(pack[1], 1), :])
            for pack in ids
        ]
        spread = [jnp.exp(jnp.where(within, c - a, -1e30)) for c, a in zip(cum, across)]
        keys = [stack(k_rows, pack).astype(BF16) for pack in ids]
        lower = [
            jnp.where(strict, dot(k, k, NT) * s, 0.0) * b for k, s, b in zip(keys, spread, beta)
        ]
        block = 8
        inner = [jnp.where(same(block), a, 0.0) for a in lower]
        inner_short = short(inner)
        inverse = [identity - a for a in inner]
        square = short([dot(a, a) for a in inner_short])
        fourth = short([dot(a, a) for a in square])
        inverse = [x + dot(y, a) for x, y, a in zip(inverse, short(inverse), square)]
        inverse = [x + dot(y, a) for x, y, a in zip(inverse, short(inverse), fourth)]
        grown = [jnp.exp(c) for c in cum]
        wide = [k.astype(F32) for k in keys]
        right = short([
            jnp.concatenate([stack(v_rows, pack) * b, w * (g * b)], axis=1)
            for pack, b, w, g in zip(ids, beta, wide, grown)
        ])
        while block < tokens:
            between = same(2 * block) & ~same(block)
            corner = short([jnp.where(between, a, 0.0) for a in lower])
            held = short(inverse)
            crossed = short([dot(x, a) for x, a in zip(held, corner)])
            block *= 2
            if block < tokens:
                inverse = [x - dot(a, y) for x, a, y in zip(inverse, crossed, held)]
        partly = [dot(x, r) for x, r in zip(held, right)]
        solved = short([y - dot(a, z) for y, a, z in zip(partly, crossed, short(partly))])
        scales = [
            jnp.where(first_head, beta_rows[pl.ds(pack[0], 1), :], beta_rows[pl.ds(pack[1], 1), :])
            for pack in ids
        ]
        solver = [
            (x - dot(a, y)) * b for x, a, y, b in zip(inverse, crossed, held, scales)
        ]
        return [
            dict(units=pack, ids=i, spread=s, keys=k, solved=x, grown=g, solver=t)
            for pack, i, s, k, x, g, t in zip(packs, ids, spread, keys, solved, grown, solver)
        ]

    def terms_copy(step):
        return pltpu.make_async_remote_copy(
            src_ref=terms_out.at[step], dst_ref=terms_in.at[me],
            send_sem=terms_send.at[step], recv_sem=terms_recv.at[step],
            device_id=partner(step), device_id_type=MESH,
        )

    def query_copy(step):
        return pltpu.make_async_remote_copy(
            src_ref=query_out.at[step], dst_ref=query_in.at[me],
            send_sem=query_send.at[step], recv_sem=query_recv.at[step],
            device_id=partner(step), device_id_type=MESH,
        )

    def solver_copy(step):
        return pltpu.make_async_remote_copy(
            src_ref=solver_out.at[step], dst_ref=solver_in.at[me],
            send_sem=solver_send.at[step], recv_sem=solver_recv.at[step],
            device_id=partner(step), device_id_type=MESH,
        )

    tail_row = lax.broadcasted_iota(jnp.int32, (16, width), 0)

    def store_terms(step):
        target = terms_in.at[me] if step == 0 else terms_out.at[step]
        tail = jnp.zeros((16, width), F32)
        for part in range(own):
            head, to = lax.rem(me + step, n_head) * own + part, part * tokens
            from_head = pl.ds(head, tokens, stride=heads)
            target[to : to + tokens, :] = k_rows[from_head, :].astype(BF16)
            target[rows + to : rows + to + tokens, :] = v_rows[from_head, :].astype(BF16)
            decay = kept_gate[1, pl.ds(head, 1), :]
            high = decay.astype(BF16).astype(F32)
            tail = jnp.where(tail_row == 3 * part, kept_gate[0, pl.ds(head, 1), :], tail)
            tail = jnp.where(tail_row == 3 * part + 1, high, tail)
            tail = jnp.where(tail_row == 3 * part + 2, decay - high, tail)
        target[2 * rows :, :] = tail.astype(BF16)
        if step:
            terms_copy(step).start()

    pairs = max(own // 2, 1)

    def store_solvers(batch):
        for data in batch:
            scaled = data["solver"]
            top, low = scaled[:tokens], scaled[tokens:]
            for at, (step, part) in enumerate(data["units"]):
                target = solver_in.at[me] if step == 0 else solver_out.at[step]
                if own == 1:
                    mine = (top, low)[at]
                    both = jnp.concatenate([mine[:, tokens:], mine[:, :tokens]], axis=1) + mine
                    target[...] = both.astype(BF16)
                elif at == 0:
                    to = part // 2 * tokens
                    target[to : to + tokens, :] = (top + low).astype(BF16)

    def query_terms(batch):
        queries = [stack(q_rows, data["ids"]).astype(BF16) for data in batch]
        scores = short([dot(q, d["keys"], NT) * d["spread"] for q, d in zip(queries, batch)])
        mixed = [dot(s, d["solved"]) for s, d in zip(scores, batch)]
        for q, m, d in zip(queries, mixed, batch):
            through = (q.astype(F32) * d["grown"] - m[:, width:]).astype(BF16)
            for at, (step, part) in enumerate(d["units"]):
                section, to = slice(at * tokens, (at + 1) * tokens), part * tokens
                target = query_in.at[me] if step == 0 else query_out.at[step]
                target[to : to + tokens, :] = through[section]
                offset[step, part] = m[section, :width]

    order = list(range(1, n_head)) + [0]
    units = [(step, part) for step in order for part in range(own)]
    packs = [units[at : at + PACK] for at in range(0, len(units), PACK)]
    pl.semaphore_wait(barrier, n_head + 1)
    for step in order:
        store_terms(step)
    loads[4].wait()
    q_rows[...] = unit(q_ref[...]) * width ** (-0.5)
    loads[5].wait()
    kept = []
    for at in range(0, len(packs), BATCH):
        batch = batch_terms(packs[at : at + BATCH])
        store_solvers(batch)
        kept.append(batch)
    for step in range(1, n_head):
        solver_copy(step).start()
    for batch in kept:
        query_terms(batch)
    for step in range(1, n_head):
        query_copy(step).start()

    for step in range(1, n_head):
        terms_copy(step).wait_recv()
    low_lane = lax.broadcasted_iota(jnp.int32, (tokens, size), 1) < tokens
    eye_t = row_t == col_t
    shrunk = []
    for group in range(n_head):
        tail = terms_in[group, 2 * rows :, :].astype(F32)
        for part in range(own):
            keys = terms_in[group, part * tokens : (part + 1) * tokens, :]
            shrink = tail[3 * part : 3 * part + 1, tokens:]
            shrunk.append(dot(jnp.where(eye_t, shrink, 0.0).astype(BF16), keys).astype(BF16))
    for step in range(1, n_head):
        solver_copy(step).wait_recv()
    erasers_of, pseudo_of = [], []
    for group in range(n_head):
        tail = terms_in[group, 2 * rows :, :].astype(F32)
        for pair in range(pairs):
            solver = solver_in[group, pair * tokens : (pair + 1) * tokens, :].astype(F32)
            many = min(own, 2)
            grows = [tail[3 * part : 3 * part + 1, :] for part in range(many * pair, many * pair + many)]
            if many == 2:
                mirrored = jnp.concatenate([grows[1][:, tokens:], grows[1][:, :tokens]], axis=1)
                grow = jnp.where(first_head, grows[0], mirrored)
                diagonal = lambda t: jnp.concatenate(
                    [jnp.where(low_lane, t, 0.0), jnp.where(low_lane, 0.0, t)], axis=0
                ).astype(BF16)
            else:
                grow = grows[0]
                diagonal = lambda t: t[:, :tokens].astype(BF16)
            section = slice(pair * many * tokens, (pair + 1) * many * tokens)
            beyond = slice(rows + section.start, rows + section.stop)
            erasers = dot(diagonal(solver * grow), terms_in[group, section, :]).astype(BF16)
            pseudo = dot(diagonal(solver), terms_in[group, beyond, :]).astype(BF16)
            for at in range(many):
                erasers_of.append(erasers[at * tokens : (at + 1) * tokens])
                pseudo_of.append(pseudo[at * tokens : (at + 1) * tokens])
    eye = jnp.where(
        lax.broadcasted_iota(jnp.int32, (width, width), 0)
        == lax.broadcasted_iota(jnp.int32, (width, width), 1), 1.0, 0.0,
    )
    current = [jnp.concatenate([eye, jnp.zeros((width, width), F32)], axis=1)] * own
    for group in range(n_head):
        tail = terms_in[group, 2 * rows :, :].astype(F32)
        held = short(current)
        for part in range(own):
            prefix[part, group] = held[part]
        for part in range(own):
            pseudo = pseudo_of[group * own + part]
            erasers = erasers_of[group * own + part]
            carried = shrunk[group * own + part]
            decay = tail[3 * part + 1 : 3 * part + 2, :] + tail[3 * part + 2 : 3 * part + 3, :]
            if group:
                erased = dot(erasers, held[part])
                change = jnp.concatenate(
                    [erased[:, :width], erased[:, width:] - pseudo.astype(F32)], axis=1
                ).astype(BF16)
            else:
                change = jnp.concatenate([erasers, -pseudo], axis=1)
            decay = jnp.concatenate([decay, decay], axis=1)
            current[part] = current[part] * decay - dot(carried, change, TN)
    for part in range(own):
        high = current[part][:, :width].astype(BF16)
        slab_high[part] = high
        slab_low[part] = (current[part][:, :width] - high.astype(F32)).astype(BF16)
        slab_add[part] = current[part][:, width:]

    def chain_copy(part):
        return pltpu.make_async_remote_copy(
            src_ref=chain_out.at[part], dst_ref=chain_in.at[part],
            send_sem=chain_send.at[part], recv_sem=chain_recv.at[part],
            device_id={"seq": lax.rem(seq + 1, n_seq)}, device_id_type=MESH,
        )

    def core_copy(step, part):
        slot = n_head - step
        group = lax.rem(me + step, n_head)
        return pltpu.make_async_remote_copy(
            src_ref=core_out.at[part, group], dst_ref=core_in.at[slot, part],
            send_sem=core_send.at[step, part], recv_sem=core_recv.at[slot, part],
            device_id=partner(step), device_id_type=MESH,
        )

    def map_queries():
        for step in range(1, n_head):
            query_copy(step).wait_recv()
        for group in range(n_head):
            for part in range(own):
                section = slice(group * tokens, (group + 1) * tokens)
                at = part * tokens
                queries = query_in[group, at : at + tokens, :]
                mapped = dot(queries, prefix[part, group])
                query_map[part, section, :] = mapped[:, :width].astype(BF16)
                query_add[part, section, :] = mapped[:, width:]

    def pass_on(part):
        @pl.when(seq > 0)
        def _():
            chain_copy(part).wait_recv()

        @pl.when(seq < n_seq - 1)
        def _():
            state = chain_in[part]
            moved = dot(slab_high[part], state) + dot(slab_low[part], state)
            chain_out[part] = (moved + slab_add[part]).astype(BF16)
            chain_copy(part).start()

    def give_cores(part):
        cores = dot(query_map[part], chain_in[part]) + query_add[part]
        core_out[part] = cores.astype(BF16).reshape(n_head, tokens, width)
        for step in range(1, n_head):
            core_copy(step, part).start()

    @pl.when(seq == 0)
    def _():
        chain_in[...] = jnp.zeros_like(chain_in)

    late = seq >= n_seq // 2

    @pl.when(late)
    def _():
        map_queries()
        for part in range(own):
            pass_on(part)
            give_cores(part)

    @pl.when(jnp.logical_not(late))
    def _():
        for part in range(own):
            pass_on(part)
        map_queries()
        for part in range(own):
            give_cores(part)

    gain = gain_ref[...]
    for step in [0] + list(range(n_head - 1, 0, -1)):
        for part in range(own):
            if step:
                core_copy(n_head - step, part).wait_recv()
                core = core_in[step, part]
            else:
                core = core_out[part, me]
            core = core.astype(F32) + offset[step, part]
            scale = lax.rsqrt(jnp.mean(core * core, axis=-1, keepdims=True) + 1e-06)
            head = lax.rem(me + step, n_head) * own + part
            out_rows[pl.ds(head, tokens, stride=heads), :] = core * scale * gain
    out_ref[...] = out_rows[...].reshape(tokens, heads, width).astype(BF16)

    for step in range(1, n_head):
        terms_copy(step).wait_send()
        solver_copy(step).wait_send()
        query_copy(step).wait_send()
        for part in range(own):
            core_copy(step, part).wait_send()

    @pl.when(seq < n_seq - 1)
    def _():
        for part in range(own):
            chain_copy(part).wait_send()


def solution(mesh):
    n_seq, n_head = mesh.shape["seq"], mesh.shape["head"]

    def local(queries, keys, values, log_decay, beta, norm_gain):
        tokens, heads, width = queries.shape
        own = heads // n_head
        length = tokens * heads
        hbm = pl.BlockSpec(memory_space=pltpu.HBM)
        payload = (n_head, 2 * own * tokens + 16, width)
        solvers = (n_head, max(own // 2, 1) * tokens, 2 * tokens)
        dma = pltpu.SemaphoreType.DMA
        return pl.pallas_call(
            functools.partial(kernel, n_seq, n_head),
            out_shape=pltpu.VMEM(queries.shape, BF16),
            in_specs=[hbm] * 6,
            out_specs=pl.BlockSpec(memory_space=pltpu.VMEM),
            scratch_shapes=[
                pltpu.VMEM(queries.shape, BF16),
                pltpu.VMEM(queries.shape, BF16),
                pltpu.VMEM(queries.shape, BF16),
                pltpu.VMEM((heads, tokens), BF16),
                pltpu.VMEM((heads, tokens), BF16),
                pltpu.VMEM((1, width), F32),
                pltpu.VMEM((length, width), F32),
                pltpu.VMEM((length, width), F32),
                pltpu.VMEM((length, width), F32),
                pltpu.VMEM((length, width), F32),
                pltpu.VMEM((heads, PACK * tokens), F32),
                pltpu.VMEM((heads, PACK * tokens), F32),
                pltpu.VMEM((2, heads, PACK * tokens), F32),
                pltpu.VMEM(payload, BF16),
                pltpu.VMEM(payload, BF16),
                pltpu.VMEM(solvers, BF16),
                pltpu.VMEM(solvers, BF16),
                pltpu.VMEM((n_head, own * tokens, width), BF16),
                pltpu.VMEM((n_head, own * tokens, width), BF16),
                pltpu.VMEM((n_head, own, tokens, width), F32),
                pltpu.VMEM((own, n_head, width, 2 * width), BF16),
                pltpu.VMEM((own, width, width), BF16),
                pltpu.VMEM((own, width, width), BF16),
                pltpu.VMEM((own, width, width), F32),
                pltpu.VMEM((own, n_head * tokens, width), BF16),
                pltpu.VMEM((own, n_head * tokens, width), F32),
                pltpu.VMEM((own, width, width), BF16),
                pltpu.VMEM((own, width, width), BF16),
                pltpu.VMEM((own, n_head, tokens, width), BF16),
                pltpu.VMEM((n_head, own, tokens, width), BF16),
                dma((6,)),
                dma((n_head,)),
                dma((n_head,)),
                dma((n_head,)),
                dma((n_head,)),
                dma((n_head,)),
                dma((n_head,)),
                dma((own,)),
                dma((own,)),
                dma((n_head, own)),
                dma((n_head, own)),
            ],
            compiler_params=pltpu.CompilerParams(
                collective_id=0, has_side_effects=True, vmem_limit_bytes=48 * 1024 * 1024
            ),
            name="gated_delta",
        )(*[
            pltpu.with_memory_space_constraint(array, pltpu.HBM)
            for array in (queries, keys, values, log_decay.T, beta.T, norm_gain.reshape(1, width))
        ])

    tokens_by_device = P(("seq", "head"), None, None)
    placed = (tokens_by_device,) * 3 + (P(("seq", "head"), None),) * 2 + (P(),)
    return jax.shard_map(
        local, mesh=mesh, in_specs=placed, out_specs=tokens_by_device, check_vma=False
    )
```

```python
import functools

import jax
import jax.numpy as jnp
from jax import lax
from jax.experimental import pallas as pl
from jax.experimental.pallas import tpu as pltpu
from jax.sharding import PartitionSpec as P

PACK = 2
BATCH = 8
MESH = pl.DeviceIdType.MESH
F32, BF16 = jnp.float32, jnp.bfloat16
NT, TN = ((1,), (1,)), ((0,), (0,))


def dot(left, right, dims=((1,), (0,))):
    return lax.dot_general(left, right, (dims, ((), ())), preferred_element_type=F32)


def short(tensors):
    return [tensor.astype(BF16) for tensor in tensors]


def unit(tensor):
    flat = tensor.astype(F32).reshape(-1, tensor.shape[-1])
    return flat * lax.rsqrt(jnp.sum(flat * flat, axis=-1, keepdims=True) + 1e-06)


def kernel(
    n_seq, n_head, q_hbm, k_hbm, v_hbm, decay_hbm, beta_hbm, gain_hbm, out_ref,
    q_ref, k_ref, v_ref, decay_ref, beta_ref, gain_ref,
    q_rows, k_rows, v_rows, out_rows, row_gate, beta_rows, kept_gate, terms_out, terms_in, solver_out, solver_in, query_out, query_in, offset,
    prefix, slab_map, slab_add, front_map, chip_map, chip_add, entry, query_map, query_add,
    chain_in, chain_out, core_out, core_in,
    load_sem, terms_send, terms_recv, solver_send, solver_recv, query_send, query_recv,
    map_send, map_recv, entry_send, entry_recv, chain_send, chain_recv, core_send, core_recv,
):
    seq, me = lax.axis_index("seq"), lax.axis_index("head")
    tokens, heads, width = q_ref.shape
    own = heads // n_head
    rows = own * tokens

    def partner(step):
        return {"head": lax.rem(me + step, n_head)}

    sources = (decay_hbm, beta_hbm, k_hbm, v_hbm, q_hbm, gain_hbm)
    targets = (decay_ref, beta_ref, k_ref, v_ref, q_ref, gain_ref)
    loads = [
        pltpu.make_async_copy(source, target, load_sem.at[at])
        for at, (source, target) in enumerate(zip(sources, targets))
    ]
    for load in loads:
        load.start()

    barrier = pltpu.get_barrier_semaphore()
    for step in range(1, n_head):
        pl.semaphore_signal(barrier, inc=1, device_id=partner(step), device_id_type=MESH)
    odd = lax.rem(seq, 2)
    mate = {"seq": seq + 1 - 2 * odd}
    for ahead in (2, n_seq - 2):
        pl.semaphore_signal(
            barrier, inc=1, device_id={"seq": lax.rem(seq + ahead, n_seq)}, device_id_type=MESH
        )
    pl.semaphore_signal(barrier, inc=1, device_id=mate, device_id_type=MESH)

    size = PACK * tokens
    row = lax.broadcasted_iota(jnp.int32, (size, size), 0)
    col = lax.broadcasted_iota(jnp.int32, (size, size), 1)

    def same(block):
        return (row // block) == (col // block)

    within = same(tokens) & (row >= col)
    strict = same(tokens) & (row > col)
    identity = jnp.where(row == col, 1.0, 0.0)
    first_head = lax.broadcasted_iota(jnp.int32, (1, size), 1) < tokens
    row_t = lax.broadcasted_iota(jnp.int32, (tokens, tokens), 0)
    col_t = lax.broadcasted_iota(jnp.int32, (tokens, tokens), 1)
    token_of = lax.rem(lax.broadcasted_iota(jnp.int32, (tokens, size), 1), tokens)
    before = lax.broadcasted_iota(jnp.int32, (tokens, size), 0) <= token_of
    lane = lax.broadcasted_iota(jnp.int32, (tokens, heads), 1)

    loads[0].wait()
    log_rows = dot(decay_ref[...], jnp.where(before, 1.0, 0.0).astype(BF16))
    row_gate[...] = log_rows
    log_end = log_rows[:, size - 1 :]
    first_half = lax.broadcasted_iota(jnp.int32, (heads, size), 1) < tokens
    kept_gate[0] = jnp.exp(jnp.where(first_half, log_rows, log_end - log_rows))
    kept_gate[1] = jnp.broadcast_to(jnp.exp(log_end), (heads, size))
    cumulative = dot(jnp.where(row_t >= col_t, 1.0, 0.0).astype(BF16), decay_ref[...], NT)
    loads[1].wait()
    row_beta = dot(beta_ref[...], jnp.where(token_of == lax.broadcasted_iota(
        jnp.int32, (tokens, size), 0), 1.0, 0.0).astype(BF16))
    beta_rows[...] = row_beta
    betas = dot(jnp.where(row_t == col_t, 1.0, 0.0).astype(BF16), beta_ref[...], NT)
    loads[2].wait()
    k_rows[...] = unit(k_ref[...])
    loads[3].wait()
    v_rows[...] = v_ref[...].astype(F32).reshape(-1, width)
    def stack(ref, ids):
        return jnp.concatenate([ref[pl.ds(i, tokens, stride=heads), :] for i in ids], axis=0)

    def column(gate, i):
        picked = jnp.sum(jnp.where(lane == i, gate, 0.0), axis=1, keepdims=True)
        return jnp.broadcast_to(picked, (tokens, width))

    def batch_terms(packs):
        ids = [[lax.rem(me + step, n_head) * own + part for step, part in pack] for pack in packs]
        cums = [[column(cumulative, i) for i in pack] for pack in ids]
        cum = [jnp.concatenate(pack, axis=0) for pack in cums]
        beta = [jnp.concatenate([column(betas, i) for i in pack], axis=0) for pack in ids]
        across = [
            jnp.where(first_head, row_gate[pl.ds(pack[0], 1), :], row_gate[pl.ds(pack[1], 1), :])
            for pack in ids
        ]
        spread = [jnp.exp(jnp.where(within, c - a, -1e30)) for c, a in zip(cum, across)]
        keys = [stack(k_rows, pack).astype(BF16) for pack in ids]
        lower = [
            jnp.where(strict, dot(k, k, NT) * s, 0.0) * b for k, s, b in zip(keys, spread, beta)
        ]
        block = 8
        inner = [jnp.where(same(block), a, 0.0) for a in lower]
        inner_short = short(inner)
        inverse = [identity - a for a in inner]
        square = short([dot(a, a) for a in inner_short])
        fourth = short([dot(a, a) for a in square])
        inverse = [x + dot(y, a) for x, y, a in zip(inverse, short(inverse), square)]
        inverse = [x + dot(y, a) for x, y, a in zip(inverse, short(inverse), fourth)]
        grown = [jnp.exp(c) for c in cum]
        wide = [k.astype(F32) for k in keys]
        right = short([
            jnp.concatenate([stack(v_rows, pack) * b, w * (g * b)], axis=1)
            for pack, b, w, g in zip(ids, beta, wide, grown)
        ])
        while block < tokens:
            between = same(2 * block) & ~same(block)
            corner = short([jnp.where(between, a, 0.0) for a in lower])
            held = short(inverse)
            crossed = short([dot(x, a) for x, a in zip(held, corner)])
            block *= 2
            if block < tokens:
                inverse = [x - dot(a, y) for x, a, y in zip(inverse, crossed, held)]
        partly = [dot(x, r) for x, r in zip(held, right)]
        solved = short([y - dot(a, z) for y, a, z in zip(partly, crossed, short(partly))])
        scales = [
            jnp.where(first_head, beta_rows[pl.ds(pack[0], 1), :], beta_rows[pl.ds(pack[1], 1), :])
            for pack in ids
        ]
        solver = [
            (x - dot(a, y)) * b for x, a, y, b in zip(inverse, crossed, held, scales)
        ]
        return [
            dict(units=pack, ids=i, spread=s, keys=k, solved=x, grown=g, solver=t)
            for pack, i, s, k, x, g, t in zip(packs, ids, spread, keys, solved, grown, solver)
        ]

    def terms_copy(step):
        return pltpu.make_async_remote_copy(
            src_ref=terms_out.at[step], dst_ref=terms_in.at[me],
            send_sem=terms_send.at[step], recv_sem=terms_recv.at[step],
            device_id=partner(step), device_id_type=MESH,
        )

    def query_copy(step):
        return pltpu.make_async_remote_copy(
            src_ref=query_out.at[step], dst_ref=query_in.at[me],
            send_sem=query_send.at[step], recv_sem=query_recv.at[step],
            device_id=partner(step), device_id_type=MESH,
        )

    def solver_copy(step):
        return pltpu.make_async_remote_copy(
            src_ref=solver_out.at[step], dst_ref=solver_in.at[me],
            send_sem=solver_send.at[step], recv_sem=solver_recv.at[step],
            device_id=partner(step), device_id_type=MESH,
        )

    tail_row = lax.broadcasted_iota(jnp.int32, (16, width), 0)

    def store_terms(step):
        target = terms_in.at[me] if step == 0 else terms_out.at[step]
        tail = jnp.zeros((16, width), F32)
        for part in range(own):
            head, to = lax.rem(me + step, n_head) * own + part, part * tokens
            from_head = pl.ds(head, tokens, stride=heads)
            target[to : to + tokens, :] = k_rows[from_head, :].astype(BF16)
            target[rows + to : rows + to + tokens, :] = v_rows[from_head, :].astype(BF16)
            decay = kept_gate[1, pl.ds(head, 1), :]
            high = decay.astype(BF16).astype(F32)
            tail = jnp.where(tail_row == 3 * part, kept_gate[0, pl.ds(head, 1), :], tail)
            tail = jnp.where(tail_row == 3 * part + 1, high, tail)
            tail = jnp.where(tail_row == 3 * part + 2, decay - high, tail)
        target[2 * rows :, :] = tail.astype(BF16)
        if step:
            terms_copy(step).start()

    pairs = max(own // 2, 1)

    def store_solvers(batch):
        for data in batch:
            scaled = data["solver"]
            top, low = scaled[:tokens], scaled[tokens:]
            for at, (step, part) in enumerate(data["units"]):
                target = solver_in.at[me] if step == 0 else solver_out.at[step]
                if own == 1:
                    mine = (top, low)[at]
                    both = jnp.concatenate([mine[:, tokens:], mine[:, :tokens]], axis=1) + mine
                    target[...] = both.astype(BF16)
                elif at == 0:
                    to = part // 2 * tokens
                    target[to : to + tokens, :] = (top + low).astype(BF16)

    def query_terms(batch):
        queries = [stack(q_rows, data["ids"]).astype(BF16) for data in batch]
        scores = short([dot(q, d["keys"], NT) * d["spread"] for q, d in zip(queries, batch)])
        mixed = [dot(s, d["solved"]) for s, d in zip(scores, batch)]
        for q, m, d in zip(queries, mixed, batch):
            through = (q.astype(F32) * d["grown"] - m[:, width:]).astype(BF16)
            for at, (step, part) in enumerate(d["units"]):
                section, to = slice(at * tokens, (at + 1) * tokens), part * tokens
                target = query_in.at[me] if step == 0 else query_out.at[step]
                target[to : to + tokens, :] = through[section]
                offset[step, part] = m[section, :width]

    order = list(range(1, n_head)) + [0]
    units = [(step, part) for step in order for part in range(own)]
    packs = [units[at : at + PACK] for at in range(0, len(units), PACK)]
    pl.semaphore_wait(barrier, n_head + 2)
    for step in order:
        store_terms(step)
    loads[4].wait()
    q_rows[...] = unit(q_ref[...]) * width ** (-0.5)
    loads[5].wait()
    kept = []
    for at in range(0, len(packs), BATCH):
        batch = batch_terms(packs[at : at + BATCH])
        store_solvers(batch)
        kept.append(batch)
    for step in range(1, n_head):
        solver_copy(step).start()
    for batch in kept:
        query_terms(batch)
    for step in range(1, n_head):
        query_copy(step).start()

    for step in range(1, n_head):
        terms_copy(step).wait_recv()
    low_lane = lax.broadcasted_iota(jnp.int32, (tokens, size), 1) < tokens
    eye_t = row_t == col_t
    shrunk = []
    for group in range(n_head):
        tail = terms_in[group, 2 * rows :, :].astype(F32)
        for part in range(own):
            keys = terms_in[group, part * tokens : (part + 1) * tokens, :]
            shrink = tail[3 * part : 3 * part + 1, tokens:]
            shrunk.append(dot(jnp.where(eye_t, shrink, 0.0).astype(BF16), keys).astype(BF16))
    for step in range(1, n_head):
        solver_copy(step).wait_recv()
    erasers_of, pseudo_of = [], []
    for group in range(n_head):
        tail = terms_in[group, 2 * rows :, :].astype(F32)
        for pair in range(pairs):
            solver = solver_in[group, pair * tokens : (pair + 1) * tokens, :].astype(F32)
            many = min(own, 2)
            grows = [tail[3 * part : 3 * part + 1, :] for part in range(many * pair, many * pair + many)]
            if many == 2:
                mirrored = jnp.concatenate([grows[1][:, tokens:], grows[1][:, :tokens]], axis=1)
                grow = jnp.where(first_head, grows[0], mirrored)
                diagonal = lambda t: jnp.concatenate(
                    [jnp.where(low_lane, t, 0.0), jnp.where(low_lane, 0.0, t)], axis=0
                ).astype(BF16)
            else:
                grow = grows[0]
                diagonal = lambda t: t[:, :tokens].astype(BF16)
            section = slice(pair * many * tokens, (pair + 1) * many * tokens)
            beyond = slice(rows + section.start, rows + section.stop)
            erasers = dot(diagonal(solver * grow), terms_in[group, section, :]).astype(BF16)
            pseudo = dot(diagonal(solver), terms_in[group, beyond, :]).astype(BF16)
            for at in range(many):
                erasers_of.append(erasers[at * tokens : (at + 1) * tokens])
                pseudo_of.append(pseudo[at * tokens : (at + 1) * tokens])
    eye = jnp.where(
        lax.broadcasted_iota(jnp.int32, (width, width), 0)
        == lax.broadcasted_iota(jnp.int32, (width, width), 1), 1.0, 0.0,
    )
    current = [jnp.concatenate([eye, jnp.zeros((width, width), F32)], axis=1)] * own
    for group in range(n_head):
        tail = terms_in[group, 2 * rows :, :].astype(F32)
        held = short(current)
        for part in range(own):
            prefix[part, group] = held[part]
        for part in range(own):
            pseudo = pseudo_of[group * own + part]
            erasers = erasers_of[group * own + part]
            carried = shrunk[group * own + part]
            decay = tail[3 * part + 1 : 3 * part + 2, :] + tail[3 * part + 2 : 3 * part + 3, :]
            if group:
                erased = dot(erasers, held[part])
                change = jnp.concatenate(
                    [erased[:, :width], erased[:, width:] - pseudo.astype(F32)], axis=1
                ).astype(BF16)
            else:
                change = jnp.concatenate([erasers, -pseudo], axis=1)
            decay = jnp.concatenate([decay, decay], axis=1)
            current[part] = current[part] * decay - dot(carried, change, TN)
    def map_copy(part):
        return pltpu.make_async_remote_copy(
            src_ref=slab_map.at[part], dst_ref=front_map.at[part],
            send_sem=map_send.at[part], recv_sem=map_recv.at[part],
            device_id=mate, device_id_type=MESH,
        )

    def entry_copy(part):
        return pltpu.make_async_remote_copy(
            src_ref=chain_in.at[part], dst_ref=entry.at[part],
            send_sem=entry_send.at[part], recv_sem=entry_recv.at[part],
            device_id=mate, device_id_type=MESH,
        )

    def chain_copy(part):
        return pltpu.make_async_remote_copy(
            src_ref=chain_out.at[part], dst_ref=chain_in.at[part],
            send_sem=chain_send.at[part], recv_sem=chain_recv.at[part],
            device_id={"seq": lax.rem(seq + 2, n_seq)}, device_id_type=MESH,
        )

    def keep(target, part, linear):
        high = linear.astype(BF16)
        target[part, 0] = high
        target[part, 1] = (linear - high.astype(F32)).astype(BF16)

    for part in range(own):
        keep(slab_map, part, current[part][:, :width])
        slab_map[part, 2] = current[part][:, width:].astype(BF16)
        slab_add[part] = current[part][:, width:]

    def core_copy(step, part):
        slot = n_head - step
        group = lax.rem(me + step, n_head)
        return pltpu.make_async_remote_copy(
            src_ref=core_out.at[part, group], dst_ref=core_in.at[slot, part],
            send_sem=core_send.at[step, part], recv_sem=core_recv.at[slot, part],
            device_id=partner(step), device_id_type=MESH,
        )

    def map_queries():
        for step in range(1, n_head):
            query_copy(step).wait_recv()
        for group in range(n_head):
            for part in range(own):
                section = slice(group * tokens, (group + 1) * tokens)
                at = part * tokens
                queries = query_in[group, at : at + tokens, :]
                mapped = dot(queries, prefix[part, group])
                query_map[part, section, :] = mapped[:, :width].astype(BF16)
                query_add[part, section, :] = mapped[:, width:]

    def give_cores(part):
        cores = dot(query_map[part], entry[part]) + query_add[part]
        core_out[part] = cores.astype(BF16).reshape(n_head, tokens, width)
        for step in range(1, n_head):
            core_copy(step, part).start()

    @pl.when(odd == 0)
    def _():
        for part in range(own):
            map_copy(part).start()
        map_queries()
        for part in range(own):
            entry_copy(part).wait_recv()
            give_cores(part)
        for part in range(own):
            map_copy(part).wait_send()

    first, last, late = seq < 2, seq >= n_seq - 2, seq >= n_seq // 2

    def compose_chip():
        for part in range(own):
            map_copy(part).wait_recv()
            high, low = slab_map[part, 0], slab_map[part, 1]
            front, front_low, front_add = (front_map[part, at] for at in range(3))
            linear = dot(high, front) + (dot(low, front) + dot(high, front_low))
            keep(chip_map, part, linear)
            chip_add[part] = dot(high, front_add) + dot(low, front_add) + slab_add[part]

    def pass_on(part):
        @pl.when(jnp.logical_not(first))
        def _():
            chain_copy(part).wait_recv()

        @pl.when(jnp.logical_not(last))
        def _():
            state = chain_in[part]
            moved = dot(chip_map[part, 0], state) + dot(chip_map[part, 1], state)
            chain_out[part] = (moved + chip_add[part]).astype(BF16)
            chain_copy(part).start()

        entry_copy(part).start()

    def enter(part):
        state = chain_in[part]
        moved = dot(front_map[part, 0], state) + dot(front_map[part, 1], state)
        entry[part] = (moved + front_map[part, 2].astype(F32)).astype(BF16)
        give_cores(part)

    @pl.when(odd == 1)
    def _():
        @pl.when(first)
        def _():
            chain_in[...] = jnp.zeros_like(chain_in)

        compose_chip()

        @pl.when(last)
        def _():
            map_queries()
            for part in range(own):
                pass_on(part)
                if part:
                    enter(part - 1)
            enter(own - 1)

        @pl.when(jnp.logical_not(last))
        def _():
            @pl.when(late)
            def _():
                map_queries()

            for part in range(own):
                pass_on(part)

            @pl.when(jnp.logical_not(late))
            def _():
                map_queries()

            for part in range(own):
                enter(part)

        for part in range(own):
            entry_copy(part).wait_send()

            @pl.when(jnp.logical_not(last))
            def _():
                chain_copy(part).wait_send()

    gain = gain_ref[...]
    for step in [0] + list(range(n_head - 1, 0, -1)):
        for part in range(own):
            if step:
                core_copy(n_head - step, part).wait_recv()
                core = core_in[step, part]
            else:
                core = core_out[part, me]
            core = core.astype(F32) + offset[step, part]
            scale = lax.rsqrt(jnp.mean(core * core, axis=-1, keepdims=True) + 1e-06)
            head = lax.rem(me + step, n_head) * own + part
            out_rows[pl.ds(head, tokens, stride=heads), :] = core * scale * gain
    out_ref[...] = out_rows[...].reshape(tokens, heads, width).astype(BF16)

    for step in range(1, n_head):
        terms_copy(step).wait_send()
        solver_copy(step).wait_send()
        query_copy(step).wait_send()
        for part in range(own):
            core_copy(step, part).wait_send()


def solution(mesh):
    n_seq, n_head = mesh.shape["seq"], mesh.shape["head"]

    def local(queries, keys, values, log_decay, beta, norm_gain):
        tokens, heads, width = queries.shape
        own = heads // n_head
        length = tokens * heads
        hbm = pl.BlockSpec(memory_space=pltpu.HBM)
        payload = (n_head, 2 * own * tokens + 16, width)
        solvers = (n_head, max(own // 2, 1) * tokens, 2 * tokens)
        dma = pltpu.SemaphoreType.DMA
        return pl.pallas_call(
            functools.partial(kernel, n_seq, n_head),
            out_shape=pltpu.VMEM(queries.shape, BF16),
            in_specs=[hbm] * 6,
            out_specs=pl.BlockSpec(memory_space=pltpu.VMEM),
            scratch_shapes=[
                pltpu.VMEM(queries.shape, BF16),
                pltpu.VMEM(queries.shape, BF16),
                pltpu.VMEM(queries.shape, BF16),
                pltpu.VMEM((heads, tokens), BF16),
                pltpu.VMEM((heads, tokens), BF16),
                pltpu.VMEM((1, width), F32),
                pltpu.VMEM((length, width), F32),
                pltpu.VMEM((length, width), F32),
                pltpu.VMEM((length, width), F32),
                pltpu.VMEM((length, width), F32),
                pltpu.VMEM((heads, PACK * tokens), F32),
                pltpu.VMEM((heads, PACK * tokens), F32),
                pltpu.VMEM((2, heads, PACK * tokens), F32),
                pltpu.VMEM(payload, BF16),
                pltpu.VMEM(payload, BF16),
                pltpu.VMEM(solvers, BF16),
                pltpu.VMEM(solvers, BF16),
                pltpu.VMEM((n_head, own * tokens, width), BF16),
                pltpu.VMEM((n_head, own * tokens, width), BF16),
                pltpu.VMEM((n_head, own, tokens, width), F32),
                pltpu.VMEM((own, n_head, width, 2 * width), BF16),
                pltpu.VMEM((own, 3, width, width), BF16),
                pltpu.VMEM((own, width, width), F32),
                pltpu.VMEM((own, 3, width, width), BF16),
                pltpu.VMEM((own, 2, width, width), BF16),
                pltpu.VMEM((own, width, width), F32),
                pltpu.VMEM((own, width, width), BF16),
                pltpu.VMEM((own, n_head * tokens, width), BF16),
                pltpu.VMEM((own, n_head * tokens, width), F32),
                pltpu.VMEM((own, width, width), BF16),
                pltpu.VMEM((own, width, width), BF16),
                pltpu.VMEM((own, n_head, tokens, width), BF16),
                pltpu.VMEM((n_head, own, tokens, width), BF16),
                dma((6,)),
                dma((n_head,)),
                dma((n_head,)),
                dma((n_head,)),
                dma((n_head,)),
                dma((n_head,)),
                dma((n_head,)),
                dma((own,)),
                dma((own,)),
                dma((own,)),
                dma((own,)),
                dma((own,)),
                dma((own,)),
                dma((n_head, own)),
                dma((n_head, own)),
            ],
            compiler_params=pltpu.CompilerParams(
                collective_id=0, has_side_effects=True, vmem_limit_bytes=48 * 1024 * 1024
            ),
            name="gated_delta",
        )(*[
            pltpu.with_memory_space_constraint(array, pltpu.HBM)
            for array in (queries, keys, values, log_decay.T, beta.T, norm_gain.reshape(1, width))
        ])

    tokens_by_device = P(("seq", "head"), None, None)
    placed = (tokens_by_device,) * 3 + (P(("seq", "head"), None),) * 2 + (P(),)
    return jax.shard_map(
        local, mesh=mesh, in_specs=placed, out_specs=tokens_by_device, check_vma=False
    )
```

```python
import functools

import jax
import jax.numpy as jnp
from jax import lax
from jax.experimental import pallas as pl
from jax.experimental.pallas import tpu as pltpu
from jax.sharding import PartitionSpec as P

PACK = 2
BATCH = 8
MESH = pl.DeviceIdType.MESH
F32, BF16 = jnp.float32, jnp.bfloat16
NT, TN = ((1,), (1,)), ((0,), (0,))


def dot(left, right, dims=((1,), (0,))):
    return lax.dot_general(left, right, (dims, ((), ())), preferred_element_type=F32)


def short(tensors):
    return [tensor.astype(BF16) for tensor in tensors]


def unit(tensor):
    flat = tensor.astype(F32).reshape(-1, tensor.shape[-1])
    return flat * lax.rsqrt(jnp.sum(flat * flat, axis=-1, keepdims=True) + 1e-06)


def kernel(
    n_seq, n_head, q_hbm, k_hbm, v_hbm, decay_hbm, beta_hbm, gain_hbm, out_ref,
    q_ref, k_ref, v_ref, decay_ref, beta_ref, gain_ref,
    q_rows, k_rows, v_rows, out_rows, row_gate, beta_rows, kept_gate, terms_out, terms_in, solver_out, solver_in, query_out, query_in, offset,
    prefix, slab_map, slab_add, front_map, chip_map, chip_add, entry, query_map, query_add,
    chain_in, chain_out, core_out, core_in,
    load_sem, terms_send, terms_recv, solver_send, solver_recv, query_send, query_recv,
    map_send, map_recv, entry_send, entry_recv, chain_send, chain_recv, core_send, core_recv,
):
    seq, me = lax.axis_index("seq"), lax.axis_index("head")
    tokens, heads, width = q_ref.shape
    own = heads // n_head
    rows = own * tokens

    def partner(step):
        return {"head": lax.rem(me + step, n_head)}

    sources = (decay_hbm, beta_hbm, k_hbm, v_hbm, q_hbm, gain_hbm)
    targets = (decay_ref, beta_ref, k_ref, v_ref, q_ref, gain_ref)
    loads = [
        pltpu.make_async_copy(source, target, load_sem.at[at])
        for at, (source, target) in enumerate(zip(sources, targets))
    ]
    for load in loads:
        load.start()

    barrier = pltpu.get_barrier_semaphore()
    for step in range(1, n_head):
        pl.semaphore_signal(barrier, inc=1, device_id=partner(step), device_id_type=MESH)
    odd = lax.rem(seq, 2)
    mate = {"seq": seq + 1 - 2 * odd}
    for ahead in (2, n_seq - 2):
        pl.semaphore_signal(
            barrier, inc=1, device_id={"seq": lax.rem(seq + ahead, n_seq)}, device_id_type=MESH
        )
    pl.semaphore_signal(barrier, inc=1, device_id=mate, device_id_type=MESH)

    size = PACK * tokens
    row = lax.broadcasted_iota(jnp.int32, (size, size), 0)
    col = lax.broadcasted_iota(jnp.int32, (size, size), 1)

    def same(block):
        return (row // block) == (col // block)

    within = same(tokens) & (row >= col)
    strict = same(tokens) & (row > col)
    identity = jnp.where(row == col, 1.0, 0.0)
    first_head = lax.broadcasted_iota(jnp.int32, (1, size), 1) < tokens
    row_t = lax.broadcasted_iota(jnp.int32, (tokens, tokens), 0)
    col_t = lax.broadcasted_iota(jnp.int32, (tokens, tokens), 1)
    token_of = lax.rem(lax.broadcasted_iota(jnp.int32, (tokens, size), 1), tokens)
    before = lax.broadcasted_iota(jnp.int32, (tokens, size), 0) <= token_of
    lane = lax.broadcasted_iota(jnp.int32, (tokens, heads), 1)

    loads[0].wait()
    log_rows = dot(decay_ref[...], jnp.where(before, 1.0, 0.0).astype(BF16))
    row_gate[...] = log_rows
    log_end = log_rows[:, size - 1 :]
    first_half = lax.broadcasted_iota(jnp.int32, (heads, size), 1) < tokens
    kept_gate[0] = jnp.exp(jnp.where(first_half, log_rows, log_end - log_rows))
    kept_gate[1] = jnp.broadcast_to(jnp.exp(log_end), (heads, size))
    cumulative = dot(jnp.where(row_t >= col_t, 1.0, 0.0).astype(BF16), decay_ref[...], NT)
    loads[1].wait()
    row_beta = dot(beta_ref[...], jnp.where(token_of == lax.broadcasted_iota(
        jnp.int32, (tokens, size), 0), 1.0, 0.0).astype(BF16))
    beta_rows[...] = row_beta
    betas = dot(jnp.where(row_t == col_t, 1.0, 0.0).astype(BF16), beta_ref[...], NT)
    loads[2].wait()
    k_rows[...] = unit(k_ref[...])
    loads[3].wait()
    v_rows[...] = v_ref[...].astype(F32).reshape(-1, width)
    def stack(ref, ids):
        return jnp.concatenate([ref[pl.ds(i, tokens, stride=heads), :] for i in ids], axis=0)

    def column(gate, i):
        picked = jnp.sum(jnp.where(lane == i, gate, 0.0), axis=1, keepdims=True)
        return jnp.broadcast_to(picked, (tokens, width))

    def batch_terms(packs):
        ids = [[lax.rem(me + step, n_head) * own + part for step, part in pack] for pack in packs]
        cums = [[column(cumulative, i) for i in pack] for pack in ids]
        cum = [jnp.concatenate(pack, axis=0) for pack in cums]
        beta = [jnp.concatenate([column(betas, i) for i in pack], axis=0) for pack in ids]
        across = [
            jnp.where(first_head, row_gate[pl.ds(pack[0], 1), :], row_gate[pl.ds(pack[1], 1), :])
            for pack in ids
        ]
        spread = [jnp.exp(jnp.where(within, c - a, -1e30)) for c, a in zip(cum, across)]
        keys = [stack(k_rows, pack).astype(BF16) for pack in ids]
        lower = [
            jnp.where(strict, dot(k, k, NT) * s, 0.0) * b for k, s, b in zip(keys, spread, beta)
        ]
        block = 8
        inner = [jnp.where(same(block), a, 0.0) for a in lower]
        inner_short = short(inner)
        inverse = [identity - a for a in inner]
        square = short([dot(a, a) for a in inner_short])
        fourth = short([dot(a, a) for a in square])
        inverse = [x + dot(y, a) for x, y, a in zip(inverse, short(inverse), square)]
        inverse = [x + dot(y, a) for x, y, a in zip(inverse, short(inverse), fourth)]
        while block < tokens:
            between = same(2 * block) & ~same(block)
            corner = short([jnp.where(between, a, 0.0) for a in lower])
            held = short(inverse)
            crossed = short([dot(x, a) for x, a in zip(held, corner)])
            block *= 2
            if block < tokens:
                inverse = [x - dot(a, y) for x, a, y in zip(inverse, crossed, held)]
        scales = [
            jnp.where(first_head, beta_rows[pl.ds(pack[0], 1), :], beta_rows[pl.ds(pack[1], 1), :])
            for pack in ids
        ]
        solver = short([
            (x - dot(a, y)) * b for x, a, y, b in zip(inverse, crossed, held, scales)
        ])
        return [
            dict(units=pack, ids=i, spread=s, keys=k, cum=c, solver=t)
            for pack, i, s, k, c, t in zip(packs, ids, spread, keys, cum, solver)
        ]

    def terms_copy(step):
        return pltpu.make_async_remote_copy(
            src_ref=terms_out.at[step], dst_ref=terms_in.at[me],
            send_sem=terms_send.at[step], recv_sem=terms_recv.at[step],
            device_id=partner(step), device_id_type=MESH,
        )

    def query_copy(step):
        return pltpu.make_async_remote_copy(
            src_ref=query_out.at[step], dst_ref=query_in.at[me],
            send_sem=query_send.at[step], recv_sem=query_recv.at[step],
            device_id=partner(step), device_id_type=MESH,
        )

    def solver_copy(step):
        return pltpu.make_async_remote_copy(
            src_ref=solver_out.at[step], dst_ref=solver_in.at[me],
            send_sem=solver_send.at[step], recv_sem=solver_recv.at[step],
            device_id=partner(step), device_id_type=MESH,
        )

    tail_row = lax.broadcasted_iota(jnp.int32, (16, width), 0)

    def store_terms(step):
        target = terms_in.at[me] if step == 0 else terms_out.at[step]
        tail = jnp.zeros((16, width), F32)
        for part in range(own):
            head, to = lax.rem(me + step, n_head) * own + part, part * tokens
            from_head = pl.ds(head, tokens, stride=heads)
            target[to : to + tokens, :] = k_rows[from_head, :].astype(BF16)
            target[rows + to : rows + to + tokens, :] = v_rows[from_head, :].astype(BF16)
            decay = kept_gate[1, pl.ds(head, 1), :]
            high = decay.astype(BF16).astype(F32)
            tail = jnp.where(tail_row == 3 * part, kept_gate[0, pl.ds(head, 1), :], tail)
            tail = jnp.where(tail_row == 3 * part + 1, high, tail)
            tail = jnp.where(tail_row == 3 * part + 2, decay - high, tail)
        target[2 * rows :, :] = tail.astype(BF16)
        if step:
            terms_copy(step).start()

    pairs = max(own // 2, 1)

    def store_solvers(batch):
        for data in batch:
            scaled = data["solver"]
            top, low = scaled[:tokens], scaled[tokens:]
            for at, (step, part) in enumerate(data["units"]):
                target = solver_in.at[me] if step == 0 else solver_out.at[step]
                if own == 1:
                    mine = (top, low)[at]
                    both = jnp.concatenate([mine[:, tokens:], mine[:, :tokens]], axis=1) + mine
                    target[...] = both
                elif at == 0:
                    to = part // 2 * tokens
                    target[to : to + tokens, :] = top + low

    def score_terms(batch):
        queries = [stack(q_rows, data["ids"]).astype(BF16) for data in batch]
        scores = short([dot(q, d["keys"], NT) * d["spread"] for q, d in zip(queries, batch)])
        grown = [jnp.exp(d["cum"]) for d in batch]
        right = [
            jnp.concatenate(
                [stack(v_rows, d["ids"]).astype(BF16), (d["keys"].astype(F32) * g).astype(BF16)],
                axis=1,
            )
            for d, g in zip(batch, grown)
        ]
        solved = short([dot(d["solver"], r) for d, r in zip(batch, right)])
        return [
            dict(units=d["units"], gated=q.astype(F32) * g, scores=c, solved=x)
            for d, q, g, c, x in zip(batch, queries, grown, scores, solved)
        ]

    def query_terms(batch):
        mixed = [dot(d["scores"], d["solved"]) for d in batch]
        for m, d in zip(mixed, batch):
            through = (d["gated"] - m[:, width:]).astype(BF16)
            for at, (step, part) in enumerate(d["units"]):
                section, to = slice(at * tokens, (at + 1) * tokens), part * tokens
                target = query_in.at[me] if step == 0 else query_out.at[step]
                target[to : to + tokens, :] = through[section]
                offset[step, part] = m[section, :width]

    order = list(range(1, n_head)) + [0]
    units = [(step, part) for step in order for part in range(own)]
    packs = [units[at : at + PACK] for at in range(0, len(units), PACK)]
    pl.semaphore_wait(barrier, n_head + 2)
    for step in order:
        store_terms(step)
    kept = []
    for at in range(0, len(packs), BATCH):
        batch = batch_terms(packs[at : at + BATCH])
        store_solvers(batch)
        kept.append(batch)
    for step in range(1, n_head):
        solver_copy(step).start()
    loads[4].wait()
    q_rows[...] = unit(q_ref[...]) * width ** (-0.5)
    loads[5].wait()
    scored = [score_terms(batch) for batch in kept]

    for step in range(1, n_head):
        terms_copy(step).wait_recv()
    low_lane = lax.broadcasted_iota(jnp.int32, (tokens, size), 1) < tokens
    eye_t = row_t == col_t
    shrunk = []
    for group in range(n_head):
        tail = terms_in[group, 2 * rows :, :].astype(F32)
        for part in range(own):
            keys = terms_in[group, part * tokens : (part + 1) * tokens, :]
            shrink = tail[3 * part : 3 * part + 1, tokens:]
            shrunk.append(dot(jnp.where(eye_t, shrink, 0.0).astype(BF16), keys).astype(BF16))
    for step in range(1, n_head):
        solver_copy(step).wait_recv()
    erasers_of, pseudo_of = [], []
    for group in range(n_head):
        tail = terms_in[group, 2 * rows :, :].astype(F32)
        for pair in range(pairs):
            solver = solver_in[group, pair * tokens : (pair + 1) * tokens, :].astype(F32)
            many = min(own, 2)
            grows = [tail[3 * part : 3 * part + 1, :] for part in range(many * pair, many * pair + many)]
            if many == 2:
                mirrored = jnp.concatenate([grows[1][:, tokens:], grows[1][:, :tokens]], axis=1)
                grow = jnp.where(first_head, grows[0], mirrored)
                diagonal = lambda t: jnp.concatenate(
                    [jnp.where(low_lane, t, 0.0), jnp.where(low_lane, 0.0, t)], axis=0
                ).astype(BF16)
            else:
                grow = grows[0]
                diagonal = lambda t: t[:, :tokens].astype(BF16)
            section = slice(pair * many * tokens, (pair + 1) * many * tokens)
            beyond = slice(rows + section.start, rows + section.stop)
            erasers = dot(diagonal(solver * grow), terms_in[group, section, :]).astype(BF16)
            pseudo = dot(diagonal(solver), terms_in[group, beyond, :]).astype(BF16)
            for at in range(many):
                erasers_of.append(erasers[at * tokens : (at + 1) * tokens])
                pseudo_of.append(pseudo[at * tokens : (at + 1) * tokens])
    eye = jnp.where(
        lax.broadcasted_iota(jnp.int32, (width, width), 0)
        == lax.broadcasted_iota(jnp.int32, (width, width), 1), 1.0, 0.0,
    )
    current = [jnp.concatenate([eye, jnp.zeros((width, width), F32)], axis=1)] * own
    for group in range(n_head):
        tail = terms_in[group, 2 * rows :, :].astype(F32)
        held = short(current)
        for part in range(own):
            prefix[part, group] = held[part]
        for part in range(own):
            pseudo = pseudo_of[group * own + part]
            erasers = erasers_of[group * own + part]
            carried = shrunk[group * own + part]
            decay = tail[3 * part + 1 : 3 * part + 2, :] + tail[3 * part + 2 : 3 * part + 3, :]
            if group:
                erased = dot(erasers, held[part])
                change = jnp.concatenate(
                    [erased[:, :width], erased[:, width:] - pseudo.astype(F32)], axis=1
                ).astype(BF16)
            else:
                change = jnp.concatenate([erasers, -pseudo], axis=1)
            decay = jnp.concatenate([decay, decay], axis=1)
            current[part] = current[part] * decay - dot(carried, change, TN)
    def map_copy(part, what):
        section = (slice(0, 2), slice(2, 3))[what]
        return pltpu.make_async_remote_copy(
            src_ref=slab_map.at[part, section], dst_ref=front_map.at[part, section],
            send_sem=map_send.at[what, part], recv_sem=map_recv.at[what, part],
            device_id=mate, device_id_type=MESH,
        )

    def entry_copy(part):
        return pltpu.make_async_remote_copy(
            src_ref=chain_in.at[part], dst_ref=entry.at[part],
            send_sem=entry_send.at[part], recv_sem=entry_recv.at[part],
            device_id=mate, device_id_type=MESH,
        )

    def chain_copy(part):
        return pltpu.make_async_remote_copy(
            src_ref=chain_out.at[part], dst_ref=chain_in.at[part],
            send_sem=chain_send.at[part], recv_sem=chain_recv.at[part],
            device_id={"seq": lax.rem(seq + 2, n_seq)}, device_id_type=MESH,
        )

    def keep(target, part, linear):
        high = linear.astype(BF16)
        target[part, 0] = high
        target[part, 1] = (linear - high.astype(F32)).astype(BF16)

    for part in range(own):
        keep(slab_map, part, current[part][:, :width])
        slab_map[part, 2] = current[part][:, width:].astype(BF16)
        slab_add[part] = current[part][:, width:]

    first, last, late = seq < 2, seq >= n_seq - 2, seq >= n_seq // 2

    @pl.when(odd == 0)
    def _():
        for part in range(own):
            map_copy(part, 1).start()

        @pl.when(jnp.logical_not(first))
        def _():
            for part in range(own):
                map_copy(part, 0).start()

    for batch in scored:
        query_terms(batch)
    for step in range(1, n_head):
        query_copy(step).start()

    def core_copy(step, part):
        slot = n_head - step
        group = lax.rem(me + step, n_head)
        return pltpu.make_async_remote_copy(
            src_ref=core_out.at[part, group], dst_ref=core_in.at[slot, part],
            send_sem=core_send.at[step, part], recv_sem=core_recv.at[slot, part],
            device_id=partner(step), device_id_type=MESH,
        )

    def map_queries():
        for step in range(1, n_head):
            query_copy(step).wait_recv()
        for group in range(n_head):
            for part in range(own):
                section = slice(group * tokens, (group + 1) * tokens)
                at = part * tokens
                queries = query_in[group, at : at + tokens, :]
                mapped = dot(queries, prefix[part, group])
                query_map[part, section, :] = mapped[:, :width].astype(BF16)
                query_add[part, section, :] = mapped[:, width:]

    def give_cores(part):
        cores = dot(query_map[part], entry[part]) + query_add[part]
        core_out[part] = cores.astype(BF16).reshape(n_head, tokens, width)
        for step in range(1, n_head):
            core_copy(step, part).start()

    def send_on(part):
        @pl.when(jnp.logical_not(last))
        def _():
            chain_copy(part).start()

    def compose_chip():
        for part in range(own):
            map_copy(part, 1).wait_recv()
            map_copy(part, 0).wait_recv()
            high, low = slab_map[part, 0], slab_map[part, 1]
            front, front_low, front_add = (front_map[part, at] for at in range(3))
            linear = dot(high, front) + (dot(low, front) + dot(high, front_low))
            keep(chip_map, part, linear)
            chip_add[part] = dot(high, front_add) + dot(low, front_add) + slab_add[part]

    def pass_on(part):
        chain_copy(part).wait_recv()

        @pl.when(jnp.logical_not(last))
        def _():
            state = chain_in[part]
            moved = dot(chip_map[part, 0], state) + dot(chip_map[part, 1], state)
            chain_out[part] = (moved + chip_add[part]).astype(BF16)
            chain_copy(part).start()

        entry_copy(part).start()

    def enter(part):
        state = chain_in[part]
        moved = dot(front_map[part, 0], state) + dot(front_map[part, 1], state)
        entry[part] = (moved + front_map[part, 2].astype(F32)).astype(BF16)
        give_cores(part)

    @pl.when(odd == 0)
    def _():
        map_queries()

        @pl.when(first)
        def _():
            entry[...] = jnp.zeros_like(entry)

        for part in range(own):
            @pl.when(jnp.logical_not(first))
            def _():
                entry_copy(part).wait_recv()

            give_cores(part)
        for part in range(own):
            map_copy(part, 1).wait_send()

            @pl.when(jnp.logical_not(first))
            def _():
                map_copy(part, 0).wait_send()

    @pl.when((odd == 1) & first)
    def _():
        for part in range(own):
            map_copy(part, 1).wait_recv()
            state = front_map[part, 2]
            entry[part] = state
            moved = dot(slab_map[part, 0], state) + dot(slab_map[part, 1], state)
            chain_out[part] = (moved + slab_add[part]).astype(BF16)
            send_on(part)
        map_queries()
        for part in range(own):
            give_cores(part)

    @pl.when((odd == 1) & jnp.logical_not(first))
    def _():
        compose_chip()

        @pl.when(last)
        def _():
            map_queries()
            for part in range(own):
                pass_on(part)
                if part:
                    enter(part - 1)
            enter(own - 1)

        @pl.when(jnp.logical_not(last))
        def _():
            @pl.when(late)
            def _():
                map_queries()

            for part in range(own):
                pass_on(part)

            @pl.when(jnp.logical_not(late))
            def _():
                map_queries()

            for part in range(own):
                enter(part)

        for part in range(own):
            entry_copy(part).wait_send()

    @pl.when((odd == 1) & jnp.logical_not(last))
    def _():
        for part in range(own):
            chain_copy(part).wait_send()

    gain = gain_ref[...]
    for step in [0] + list(range(n_head - 1, 0, -1)):
        for part in range(own):
            if step:
                core_copy(n_head - step, part).wait_recv()
                core = core_in[step, part]
            else:
                core = core_out[part, me]
            core = core.astype(F32) + offset[step, part]
            scale = lax.rsqrt(jnp.mean(core * core, axis=-1, keepdims=True) + 1e-06)
            head = lax.rem(me + step, n_head) * own + part
            out_rows[pl.ds(head, tokens, stride=heads), :] = core * scale * gain
    out_ref[...] = out_rows[...].reshape(tokens, heads, width).astype(BF16)

    for step in range(1, n_head):
        terms_copy(step).wait_send()
        solver_copy(step).wait_send()
        query_copy(step).wait_send()
        for part in range(own):
            core_copy(step, part).wait_send()


def solution(mesh):
    n_seq, n_head = mesh.shape["seq"], mesh.shape["head"]

    def local(queries, keys, values, log_decay, beta, norm_gain):
        tokens, heads, width = queries.shape
        own = heads // n_head
        length = tokens * heads
        hbm = pl.BlockSpec(memory_space=pltpu.HBM)
        payload = (n_head, 2 * own * tokens + 16, width)
        solvers = (n_head, max(own // 2, 1) * tokens, 2 * tokens)
        dma = pltpu.SemaphoreType.DMA
        return pl.pallas_call(
            functools.partial(kernel, n_seq, n_head),
            out_shape=pltpu.VMEM(queries.shape, BF16),
            in_specs=[hbm] * 6,
            out_specs=pl.BlockSpec(memory_space=pltpu.VMEM),
            scratch_shapes=[
                pltpu.VMEM(queries.shape, BF16),
                pltpu.VMEM(queries.shape, BF16),
                pltpu.VMEM(queries.shape, BF16),
                pltpu.VMEM((heads, tokens), BF16),
                pltpu.VMEM((heads, tokens), BF16),
                pltpu.VMEM((1, width), F32),
                pltpu.VMEM((length, width), F32),
                pltpu.VMEM((length, width), F32),
                pltpu.VMEM((length, width), F32),
                pltpu.VMEM((length, width), F32),
                pltpu.VMEM((heads, PACK * tokens), F32),
                pltpu.VMEM((heads, PACK * tokens), F32),
                pltpu.VMEM((2, heads, PACK * tokens), F32),
                pltpu.VMEM(payload, BF16),
                pltpu.VMEM(payload, BF16),
                pltpu.VMEM(solvers, BF16),
                pltpu.VMEM(solvers, BF16),
                pltpu.VMEM((n_head, own * tokens, width), BF16),
                pltpu.VMEM((n_head, own * tokens, width), BF16),
                pltpu.VMEM((n_head, own, tokens, width), F32),
                pltpu.VMEM((own, n_head, width, 2 * width), BF16),
                pltpu.VMEM((own, 3, width, width), BF16),
                pltpu.VMEM((own, width, width), F32),
                pltpu.VMEM((own, 3, width, width), BF16),
                pltpu.VMEM((own, 2, width, width), BF16),
                pltpu.VMEM((own, width, width), F32),
                pltpu.VMEM((own, width, width), BF16),
                pltpu.VMEM((own, n_head * tokens, width), BF16),
                pltpu.VMEM((own, n_head * tokens, width), F32),
                pltpu.VMEM((own, width, width), BF16),
                pltpu.VMEM((own, width, width), BF16),
                pltpu.VMEM((own, n_head, tokens, width), BF16),
                pltpu.VMEM((n_head, own, tokens, width), BF16),
                dma((6,)),
                dma((n_head,)),
                dma((n_head,)),
                dma((n_head,)),
                dma((n_head,)),
                dma((n_head,)),
                dma((n_head,)),
                dma((2, own)),
                dma((2, own)),
                dma((own,)),
                dma((own,)),
                dma((own,)),
                dma((own,)),
                dma((n_head, own)),
                dma((n_head, own)),
            ],
            compiler_params=pltpu.CompilerParams(
                collective_id=0, has_side_effects=True, vmem_limit_bytes=48 * 1024 * 1024
            ),
            name="gated_delta",
        )(*[
            pltpu.with_memory_space_constraint(array, pltpu.HBM)
            for array in (queries, keys, values, log_decay.T, beta.T, norm_gain.reshape(1, width))
        ])

    tokens_by_device = P(("seq", "head"), None, None)
    placed = (tokens_by_device,) * 3 + (P(("seq", "head"), None),) * 2 + (P(),)
    return jax.shard_map(
        local, mesh=mesh, in_specs=placed, out_specs=tokens_by_device, check_vma=False
    )
```

```python
import functools

import jax
import jax.numpy as jnp
from jax import lax
from jax.experimental import pallas as pl
from jax.experimental.pallas import tpu as pltpu
from jax.sharding import PartitionSpec as P

PACK = 2
BATCH = 8
MESH = pl.DeviceIdType.MESH
F32, BF16 = jnp.float32, jnp.bfloat16
NT, TN = ((1,), (1,)), ((0,), (0,))


def dot(left, right, dims=((1,), (0,))):
    return lax.dot_general(left, right, (dims, ((), ())), preferred_element_type=F32)


def short(tensors):
    return [tensor.astype(BF16) for tensor in tensors]


def unit(tensor):
    flat = tensor.astype(F32).reshape(-1, tensor.shape[-1])
    return flat * lax.rsqrt(jnp.sum(flat * flat, axis=-1, keepdims=True) + 1e-06)


def kernel(
    n_seq, n_head, q_hbm, k_hbm, v_hbm, decay_hbm, beta_hbm, gain_hbm, out_ref,
    q_ref, k_ref, v_ref, decay_ref, beta_ref, gain_ref,
    q_rows, k_rows, v_rows, out_rows, row_gate, beta_rows, kept_gate, terms_out, terms_in, solver_out, solver_in, query_out, query_in, offset,
    prefix, slab_map, slab_add, front_map, chip_map, chip_add, entry, query_map, query_add,
    chain_in, chain_out, core_out, core_in,
    load_sem, terms_send, terms_recv, solver_send, solver_recv, query_send, query_recv,
    map_send, map_recv, entry_send, entry_recv, chain_send, chain_recv, core_send, core_recv,
):
    seq, me = lax.axis_index("seq"), lax.axis_index("head")
    tokens, heads, width = q_ref.shape
    own = heads // n_head
    rows = own * tokens

    def partner(step):
        return {"head": lax.rem(me + step, n_head)}

    sources = (v_hbm, k_hbm, decay_hbm, beta_hbm, q_hbm, gain_hbm)
    targets = (v_ref, k_ref, decay_ref, beta_ref, q_ref, gain_ref)
    loads = [
        pltpu.make_async_copy(source, target, load_sem.at[at])
        for at, (source, target) in enumerate(zip(sources, targets))
    ]
    for load in loads:
        load.start()

    barrier = pltpu.get_barrier_semaphore()
    for step in range(1, n_head):
        pl.semaphore_signal(barrier, inc=1, device_id=partner(step), device_id_type=MESH)
    odd = lax.rem(seq, 2)
    mate = {"seq": seq + 1 - 2 * odd}
    for ahead in (2, n_seq - 2):
        pl.semaphore_signal(
            barrier, inc=1, device_id={"seq": lax.rem(seq + ahead, n_seq)}, device_id_type=MESH
        )
    pl.semaphore_signal(barrier, inc=1, device_id=mate, device_id_type=MESH)

    size = PACK * tokens
    row = lax.broadcasted_iota(jnp.int32, (size, size), 0)
    col = lax.broadcasted_iota(jnp.int32, (size, size), 1)

    def same(block):
        return (row // block) == (col // block)

    within = same(tokens) & (row >= col)
    strict = same(tokens) & (row > col)
    identity = jnp.where(row == col, 1.0, 0.0)
    first_head = lax.broadcasted_iota(jnp.int32, (1, size), 1) < tokens
    row_t = lax.broadcasted_iota(jnp.int32, (tokens, tokens), 0)
    col_t = lax.broadcasted_iota(jnp.int32, (tokens, tokens), 1)
    token_of = lax.rem(lax.broadcasted_iota(jnp.int32, (tokens, size), 1), tokens)
    before = lax.broadcasted_iota(jnp.int32, (tokens, size), 0) <= token_of
    lane = lax.broadcasted_iota(jnp.int32, (tokens, heads), 1)

    def stack(ref, ids):
        return jnp.concatenate([ref[pl.ds(i, tokens, stride=heads), :] for i in ids], axis=0)

    def held_rows(first_row, pack):
        kept_rows = []
        for step, part in pack:
            source = terms_in.at[me] if step == 0 else terms_out.at[step]
            kept_rows.append(source[first_row + part * tokens : first_row + (part + 1) * tokens, :])
        return jnp.concatenate(kept_rows, axis=0)

    def column(gate, i):
        picked = jnp.sum(jnp.where(lane == i, gate, 0.0), axis=1, keepdims=True)
        return jnp.broadcast_to(picked, (tokens, width))

    def batch_terms(packs):
        ids = [[lax.rem(me + step, n_head) * own + part for step, part in pack] for pack in packs]
        cums = [[column(cumulative, i) for i in pack] for pack in ids]
        cum = [jnp.concatenate(pack, axis=0) for pack in cums]
        beta = [jnp.concatenate([column(betas, i) for i in pack], axis=0) for pack in ids]
        across = [
            jnp.where(first_head, row_gate[pl.ds(pack[0], 1), :], row_gate[pl.ds(pack[1], 1), :])
            for pack in ids
        ]
        spread = [jnp.exp(jnp.where(within, c - a, -1e30)) for c, a in zip(cum, across)]
        keys = [held_rows(rows, pack) for pack in packs]
        lower = [
            jnp.where(strict, dot(k, k, NT) * s, 0.0) * b for k, s, b in zip(keys, spread, beta)
        ]
        block = 8
        inner = [jnp.where(same(block), a, 0.0) for a in lower]
        inner_short = short(inner)
        inverse = [identity - a for a in inner]
        square = short([dot(a, a) for a in inner_short])
        fourth = short([dot(a, a) for a in square])
        inverse = [x + dot(y, a) for x, y, a in zip(inverse, short(inverse), square)]
        inverse = [x + dot(y, a) for x, y, a in zip(inverse, short(inverse), fourth)]
        while block < tokens:
            between = same(2 * block) & ~same(block)
            corner = short([jnp.where(between, a, 0.0) for a in lower])
            held = short(inverse)
            crossed = short([dot(x, a) for x, a in zip(held, corner)])
            block *= 2
            if block < tokens:
                inverse = [x - dot(a, y) for x, a, y in zip(inverse, crossed, held)]
        scales = [
            jnp.where(first_head, beta_rows[pl.ds(pack[0], 1), :], beta_rows[pl.ds(pack[1], 1), :])
            for pack in ids
        ]
        solver = short([
            (x - dot(a, y)) * b for x, a, y, b in zip(inverse, crossed, held, scales)
        ])
        return [
            dict(units=pack, ids=i, spread=s, keys=k, cum=c, solver=t)
            for pack, i, s, k, c, t in zip(packs, ids, spread, keys, cum, solver)
        ]

    def terms_copy(step, what):
        section = (slice(0, rows), slice(rows, 2 * rows + 16))[what]
        return pltpu.make_async_remote_copy(
            src_ref=terms_out.at[step, section], dst_ref=terms_in.at[me, section],
            send_sem=terms_send.at[what, step], recv_sem=terms_recv.at[what, step],
            device_id=partner(step), device_id_type=MESH,
        )

    def query_copy(step):
        return pltpu.make_async_remote_copy(
            src_ref=query_out.at[step], dst_ref=query_in.at[me],
            send_sem=query_send.at[step], recv_sem=query_recv.at[step],
            device_id=partner(step), device_id_type=MESH,
        )

    def solver_copy(step):
        return pltpu.make_async_remote_copy(
            src_ref=solver_out.at[step], dst_ref=solver_in.at[me],
            send_sem=solver_send.at[step], recv_sem=solver_recv.at[step],
            device_id=partner(step), device_id_type=MESH,
        )

    tail_row = lax.broadcasted_iota(jnp.int32, (16, width), 0)

    def store_values(step):
        target = terms_in.at[me] if step == 0 else terms_out.at[step]
        for part in range(own):
            head, to = lax.rem(me + step, n_head) * own + part, part * tokens
            from_head = pl.ds(head, tokens, stride=heads)
            target[to : to + tokens, :] = v_rows[from_head, :].astype(BF16)
        if step:
            terms_copy(step, 0).start()

    def store_keys(step):
        target = terms_in.at[me] if step == 0 else terms_out.at[step]
        tail = jnp.zeros((16, width), F32)
        for part in range(own):
            head, to = lax.rem(me + step, n_head) * own + part, part * tokens
            from_head = pl.ds(head, tokens, stride=heads)
            target[rows + to : rows + to + tokens, :] = k_rows[from_head, :].astype(BF16)
            decay = kept_gate[1, pl.ds(head, 1), :]
            high = decay.astype(BF16).astype(F32)
            tail = jnp.where(tail_row == 3 * part, kept_gate[0, pl.ds(head, 1), :], tail)
            tail = jnp.where(tail_row == 3 * part + 1, high, tail)
            tail = jnp.where(tail_row == 3 * part + 2, decay - high, tail)
        target[2 * rows :, :] = tail.astype(BF16)
        if step:
            terms_copy(step, 1).start()

    pairs = max(own // 2, 1)

    def store_solvers(batch):
        for data in batch:
            scaled = data["solver"]
            top, low = scaled[:tokens], scaled[tokens:]
            for at, (step, part) in enumerate(data["units"]):
                target = solver_in.at[me] if step == 0 else solver_out.at[step]
                if own == 1:
                    mine = (top, low)[at]
                    both = jnp.concatenate([mine[:, tokens:], mine[:, :tokens]], axis=1) + mine
                    target[...] = both
                elif at == 0:
                    to = part // 2 * tokens
                    target[to : to + tokens, :] = top + low

    def score_terms(batch):
        queries = [stack(q_rows, data["ids"]).astype(BF16) for data in batch]
        scores = short([dot(q, d["keys"], NT) * d["spread"] for q, d in zip(queries, batch)])
        grown = [jnp.exp(d["cum"]) for d in batch]
        right = [
            jnp.concatenate(
                [held_rows(0, d["units"]), (d["keys"].astype(F32) * g).astype(BF16)],
                axis=1,
            )
            for d, g in zip(batch, grown)
        ]
        solved = short([dot(d["solver"], r) for d, r in zip(batch, right)])
        return [
            dict(units=d["units"], gated=q.astype(F32) * g, scores=c, solved=x)
            for d, q, g, c, x in zip(batch, queries, grown, scores, solved)
        ]

    def query_terms(batch):
        mixed = [dot(d["scores"], d["solved"]) for d in batch]
        for m, d in zip(mixed, batch):
            through = (d["gated"] - m[:, width:]).astype(BF16)
            for at, (step, part) in enumerate(d["units"]):
                section, to = slice(at * tokens, (at + 1) * tokens), part * tokens
                target = query_in.at[me] if step == 0 else query_out.at[step]
                target[to : to + tokens, :] = through[section]
                offset[step, part] = m[section, :width]

    order = list(range(1, n_head)) + [0]
    units = [(step, part) for step in order for part in range(own)]
    packs = [units[at : at + PACK] for at in range(0, len(units), PACK)]
    loads[0].wait()
    v_rows[...] = v_ref[...].astype(F32).reshape(-1, width)
    pl.semaphore_wait(barrier, n_head + 2)
    for step in order:
        store_values(step)
    loads[2].wait()
    log_rows = dot(decay_ref[...], jnp.where(before, 1.0, 0.0).astype(BF16))
    row_gate[...] = log_rows
    log_end = log_rows[:, size - 1 :]
    first_half = lax.broadcasted_iota(jnp.int32, (heads, size), 1) < tokens
    kept_gate[0] = jnp.exp(jnp.where(first_half, log_rows, log_end - log_rows))
    kept_gate[1] = jnp.broadcast_to(jnp.exp(log_end), (heads, size))
    cumulative = dot(jnp.where(row_t >= col_t, 1.0, 0.0).astype(BF16), decay_ref[...], NT)
    loads[3].wait()
    row_beta = dot(beta_ref[...], jnp.where(token_of == lax.broadcasted_iota(
        jnp.int32, (tokens, size), 0), 1.0, 0.0).astype(BF16))
    beta_rows[...] = row_beta
    betas = dot(jnp.where(row_t == col_t, 1.0, 0.0).astype(BF16), beta_ref[...], NT)
    loads[1].wait()
    k_rows[...] = unit(k_ref[...])
    for step in order:
        store_keys(step)
    kept = []
    for at in range(0, len(packs), BATCH):
        batch = batch_terms(packs[at : at + BATCH])
        store_solvers(batch)
        kept.append(batch)
    for step in range(1, n_head):
        solver_copy(step).start()
    loads[4].wait()
    q_rows[...] = unit(q_ref[...]) * width ** (-0.5)
    loads[5].wait()
    scored = [score_terms(batch) for batch in kept]

    for step in range(1, n_head):
        terms_copy(step, 0).wait_recv()
        terms_copy(step, 1).wait_recv()
    low_lane = lax.broadcasted_iota(jnp.int32, (tokens, size), 1) < tokens
    eye_t = row_t == col_t
    shrunk = []
    for group in range(n_head):
        tail = terms_in[group, 2 * rows :, :].astype(F32)
        for part in range(own):
            keys = terms_in[group, rows + part * tokens : rows + (part + 1) * tokens, :]
            shrink = tail[3 * part : 3 * part + 1, tokens:]
            shrunk.append(dot(jnp.where(eye_t, shrink, 0.0).astype(BF16), keys).astype(BF16))
    for step in range(1, n_head):
        solver_copy(step).wait_recv()
    erasers_of, pseudo_of = [], []
    for group in range(n_head):
        tail = terms_in[group, 2 * rows :, :].astype(F32)
        for pair in range(pairs):
            solver = solver_in[group, pair * tokens : (pair + 1) * tokens, :].astype(F32)
            many = min(own, 2)
            grows = [tail[3 * part : 3 * part + 1, :] for part in range(many * pair, many * pair + many)]
            if many == 2:
                mirrored = jnp.concatenate([grows[1][:, tokens:], grows[1][:, :tokens]], axis=1)
                grow = jnp.where(first_head, grows[0], mirrored)
                diagonal = lambda t: jnp.concatenate(
                    [jnp.where(low_lane, t, 0.0), jnp.where(low_lane, 0.0, t)], axis=0
                ).astype(BF16)
            else:
                grow = grows[0]
                diagonal = lambda t: t[:, :tokens].astype(BF16)
            section = slice(pair * many * tokens, (pair + 1) * many * tokens)
            beyond = slice(rows + section.start, rows + section.stop)
            erasers = dot(diagonal(solver * grow), terms_in[group, beyond, :]).astype(BF16)
            pseudo = dot(diagonal(solver), terms_in[group, section, :]).astype(BF16)
            for at in range(many):
                erasers_of.append(erasers[at * tokens : (at + 1) * tokens])
                pseudo_of.append(pseudo[at * tokens : (at + 1) * tokens])
    eye = jnp.where(
        lax.broadcasted_iota(jnp.int32, (width, width), 0)
        == lax.broadcasted_iota(jnp.int32, (width, width), 1), 1.0, 0.0,
    )
    current = [jnp.concatenate([eye, jnp.zeros((width, width), F32)], axis=1)] * own
    for group in range(n_head):
        tail = terms_in[group, 2 * rows :, :].astype(F32)
        held = short(current)
        for part in range(own):
            prefix[part, group] = held[part]
        for part in range(own):
            pseudo = pseudo_of[group * own + part]
            erasers = erasers_of[group * own + part]
            carried = shrunk[group * own + part]
            decay = tail[3 * part + 1 : 3 * part + 2, :] + tail[3 * part + 2 : 3 * part + 3, :]
            if group:
                erased = dot(erasers, held[part])
                change = jnp.concatenate(
                    [erased[:, :width], erased[:, width:] - pseudo.astype(F32)], axis=1
                ).astype(BF16)
            else:
                change = jnp.concatenate([erasers, -pseudo], axis=1)
            decay = jnp.concatenate([decay, decay], axis=1)
            current[part] = current[part] * decay - dot(carried, change, TN)
    def map_copy(part, what):
        section = (slice(0, 2), slice(2, 3))[what]
        return pltpu.make_async_remote_copy(
            src_ref=slab_map.at[part, section], dst_ref=front_map.at[part, section],
            send_sem=map_send.at[what, part], recv_sem=map_recv.at[what, part],
            device_id=mate, device_id_type=MESH,
        )

    def entry_copy(part):
        return pltpu.make_async_remote_copy(
            src_ref=chain_in.at[part], dst_ref=entry.at[part],
            send_sem=entry_send.at[part], recv_sem=entry_recv.at[part],
            device_id=mate, device_id_type=MESH,
        )

    def chain_copy(part):
        return pltpu.make_async_remote_copy(
            src_ref=chain_out.at[part], dst_ref=chain_in.at[part],
            send_sem=chain_send.at[part], recv_sem=chain_recv.at[part],
            device_id={"seq": lax.rem(seq + 2, n_seq)}, device_id_type=MESH,
        )

    def keep(target, part, linear):
        high = linear.astype(BF16)
        target[part, 0] = high
        target[part, 1] = (linear - high.astype(F32)).astype(BF16)

    for part in range(own):
        keep(slab_map, part, current[part][:, :width])
        slab_map[part, 2] = current[part][:, width:].astype(BF16)
        slab_add[part] = current[part][:, width:]

    first, last, late = seq < 2, seq >= n_seq - 2, seq >= n_seq // 2

    @pl.when(odd == 0)
    def _():
        for part in range(own):
            map_copy(part, 1).start()

        @pl.when(jnp.logical_not(first))
        def _():
            for part in range(own):
                map_copy(part, 0).start()

    for batch in scored:
        query_terms(batch)
    for step in range(1, n_head):
        query_copy(step).start()

    def core_copy(step, part):
        slot = n_head - step
        group = lax.rem(me + step, n_head)
        return pltpu.make_async_remote_copy(
            src_ref=core_out.at[part, group], dst_ref=core_in.at[slot, part],
            send_sem=core_send.at[step, part], recv_sem=core_recv.at[slot, part],
            device_id=partner(step), device_id_type=MESH,
        )

    def map_queries():
        for step in range(1, n_head):
            query_copy(step).wait_recv()
        for group in range(n_head):
            for part in range(own):
                section = slice(group * tokens, (group + 1) * tokens)
                at = part * tokens
                queries = query_in[group, at : at + tokens, :]
                mapped = dot(queries, prefix[part, group])
                query_map[part, section, :] = mapped[:, :width].astype(BF16)
                query_add[part, section, :] = mapped[:, width:]

    def give_cores(part):
        cores = dot(query_map[part], entry[part]) + query_add[part]
        core_out[part] = cores.astype(BF16).reshape(n_head, tokens, width)
        for step in range(1, n_head):
            core_copy(step, part).start()

    def send_on(part):
        @pl.when(jnp.logical_not(last))
        def _():
            chain_copy(part).start()

    def compose_chip():
        for part in range(own):
            map_copy(part, 1).wait_recv()
            map_copy(part, 0).wait_recv()
            high, low = slab_map[part, 0], slab_map[part, 1]
            front, front_low, front_add = (front_map[part, at] for at in range(3))
            linear = dot(high, front) + (dot(low, front) + dot(high, front_low))
            keep(chip_map, part, linear)
            chip_add[part] = dot(high, front_add) + dot(low, front_add) + slab_add[part]

    def pass_on(part):
        chain_copy(part).wait_recv()

        @pl.when(jnp.logical_not(last))
        def _():
            state = chain_in[part]
            moved = dot(chip_map[part, 0], state) + dot(chip_map[part, 1], state)
            chain_out[part] = (moved + chip_add[part]).astype(BF16)
            chain_copy(part).start()

        entry_copy(part).start()

    def enter(part):
        state = chain_in[part]
        moved = dot(front_map[part, 0], state) + dot(front_map[part, 1], state)
        entry[part] = (moved + front_map[part, 2].astype(F32)).astype(BF16)
        give_cores(part)

    @pl.when(odd == 0)
    def _():
        map_queries()

        @pl.when(first)
        def _():
            entry[...] = jnp.zeros_like(entry)

        for part in range(own):
            @pl.when(jnp.logical_not(first))
            def _():
                entry_copy(part).wait_recv()

            give_cores(part)
        for part in range(own):
            map_copy(part, 1).wait_send()

            @pl.when(jnp.logical_not(first))
            def _():
                map_copy(part, 0).wait_send()

    @pl.when((odd == 1) & first)
    def _():
        for part in range(own):
            map_copy(part, 1).wait_recv()
            state = front_map[part, 2]
            entry[part] = state
            moved = dot(slab_map[part, 0], state) + dot(slab_map[part, 1], state)
            chain_out[part] = (moved + slab_add[part]).astype(BF16)
            send_on(part)
        map_queries()
        for part in range(own):
            give_cores(part)

    @pl.when((odd == 1) & jnp.logical_not(first))
    def _():
        compose_chip()

        @pl.when(last)
        def _():
            map_queries()
            for part in range(own):
                pass_on(part)
                if part:
                    enter(part - 1)
            enter(own - 1)

        @pl.when(jnp.logical_not(last))
        def _():
            @pl.when(late)
            def _():
                map_queries()

            for part in range(own):
                pass_on(part)

            @pl.when(jnp.logical_not(late))
            def _():
                map_queries()

            for part in range(own):
                enter(part)

        for part in range(own):
            entry_copy(part).wait_send()

    @pl.when((odd == 1) & jnp.logical_not(last))
    def _():
        for part in range(own):
            chain_copy(part).wait_send()

    gain = gain_ref[...]
    for step in [0] + list(range(n_head - 1, 0, -1)):
        for part in range(own):
            if step:
                core_copy(n_head - step, part).wait_recv()
                core = core_in[step, part]
            else:
                core = core_out[part, me]
            core = core.astype(F32) + offset[step, part]
            scale = lax.rsqrt(jnp.mean(core * core, axis=-1, keepdims=True) + 1e-06)
            head = lax.rem(me + step, n_head) * own + part
            out_rows[pl.ds(head, tokens, stride=heads), :] = core * scale * gain
    out_ref[...] = out_rows[...].reshape(tokens, heads, width).astype(BF16)

    for step in range(1, n_head):
        terms_copy(step, 0).wait_send()
        terms_copy(step, 1).wait_send()
        solver_copy(step).wait_send()
        query_copy(step).wait_send()
        for part in range(own):
            core_copy(step, part).wait_send()


def solution(mesh):
    n_seq, n_head = mesh.shape["seq"], mesh.shape["head"]

    def local(queries, keys, values, log_decay, beta, norm_gain):
        tokens, heads, width = queries.shape
        own = heads // n_head
        length = tokens * heads
        hbm = pl.BlockSpec(memory_space=pltpu.HBM)
        payload = (n_head, 2 * own * tokens + 16, width)
        solvers = (n_head, max(own // 2, 1) * tokens, 2 * tokens)
        dma = pltpu.SemaphoreType.DMA
        return pl.pallas_call(
            functools.partial(kernel, n_seq, n_head),
            out_shape=pltpu.VMEM(queries.shape, BF16),
            in_specs=[hbm] * 6,
            out_specs=pl.BlockSpec(memory_space=pltpu.VMEM),
            scratch_shapes=[
                pltpu.VMEM(queries.shape, BF16),
                pltpu.VMEM(queries.shape, BF16),
                pltpu.VMEM(queries.shape, BF16),
                pltpu.VMEM((heads, tokens), BF16),
                pltpu.VMEM((heads, tokens), BF16),
                pltpu.VMEM((1, width), F32),
                pltpu.VMEM((length, width), F32),
                pltpu.VMEM((length, width), F32),
                pltpu.VMEM((length, width), F32),
                pltpu.VMEM((length, width), F32),
                pltpu.VMEM((heads, PACK * tokens), F32),
                pltpu.VMEM((heads, PACK * tokens), F32),
                pltpu.VMEM((2, heads, PACK * tokens), F32),
                pltpu.VMEM(payload, BF16),
                pltpu.VMEM(payload, BF16),
                pltpu.VMEM(solvers, BF16),
                pltpu.VMEM(solvers, BF16),
                pltpu.VMEM((n_head, own * tokens, width), BF16),
                pltpu.VMEM((n_head, own * tokens, width), BF16),
                pltpu.VMEM((n_head, own, tokens, width), F32),
                pltpu.VMEM((own, n_head, width, 2 * width), BF16),
                pltpu.VMEM((own, 3, width, width), BF16),
                pltpu.VMEM((own, width, width), F32),
                pltpu.VMEM((own, 3, width, width), BF16),
                pltpu.VMEM((own, 2, width, width), BF16),
                pltpu.VMEM((own, width, width), F32),
                pltpu.VMEM((own, width, width), BF16),
                pltpu.VMEM((own, n_head * tokens, width), BF16),
                pltpu.VMEM((own, n_head * tokens, width), F32),
                pltpu.VMEM((own, width, width), BF16),
                pltpu.VMEM((own, width, width), BF16),
                pltpu.VMEM((own, n_head, tokens, width), BF16),
                pltpu.VMEM((n_head, own, tokens, width), BF16),
                dma((6,)),
                dma((2, n_head)),
                dma((2, n_head)),
                dma((n_head,)),
                dma((n_head,)),
                dma((n_head,)),
                dma((n_head,)),
                dma((2, own)),
                dma((2, own)),
                dma((own,)),
                dma((own,)),
                dma((own,)),
                dma((own,)),
                dma((n_head, own)),
                dma((n_head, own)),
            ],
            compiler_params=pltpu.CompilerParams(
                collective_id=0, has_side_effects=True, vmem_limit_bytes=48 * 1024 * 1024
            ),
            name="gated_delta",
        )(*[
            pltpu.with_memory_space_constraint(array, pltpu.HBM)
            for array in (queries, keys, values, log_decay.T, beta.T, norm_gain.reshape(1, width))
        ])

    tokens_by_device = P(("seq", "head"), None, None)
    placed = (tokens_by_device,) * 3 + (P(("seq", "head"), None),) * 2 + (P(),)
    return jax.shard_map(
        local, mesh=mesh, in_specs=placed, out_specs=tokens_by_device, check_vma=False
    )
```

```python
import functools

import jax
import jax.numpy as jnp
from jax import lax
from jax.experimental import pallas as pl
from jax.experimental.pallas import tpu as pltpu
from jax.sharding import PartitionSpec as P

PACK = 2
BATCH = 8
MESH = pl.DeviceIdType.MESH
F32, BF16 = jnp.float32, jnp.bfloat16
NT, TN = ((1,), (1,)), ((0,), (0,))


def dot(left, right, dims=((1,), (0,))):
    return lax.dot_general(left, right, (dims, ((), ())), preferred_element_type=F32)


def short(tensors):
    return [tensor.astype(BF16) for tensor in tensors]


def unit(tensor):
    flat = tensor.astype(F32).reshape(-1, tensor.shape[-1])
    return flat * lax.rsqrt(jnp.sum(flat * flat, axis=-1, keepdims=True) + 1e-06)


def kernel(
    n_seq, n_head, q_hbm, k_hbm, v_hbm, decay_hbm, beta_hbm, gain_hbm, out_ref,
    q_ref, k_ref, v_ref, decay_ref, beta_ref, gain_ref,
    q_rows, k_rows, v_rows, out_rows, row_gate, beta_rows, kept_gate, terms_out, terms_in, solver_out, solver_in, query_out, query_in, offset,
    prefix, slab_map, slab_add, front_map, chip_map, chip_add, entry, query_map, query_add,
    chain_in, chain_out, core_out, core_in,
    load_sem, terms_send, terms_recv, solver_send, solver_recv, query_send, query_recv,
    map_send, map_recv, entry_send, entry_recv, chain_send, chain_recv, core_send, core_recv,
):
    seq, me = lax.axis_index("seq"), lax.axis_index("head")
    tokens, heads, width = q_ref.shape
    own = heads // n_head
    rows = own * tokens

    def partner(step):
        return {"head": lax.rem(me + step, n_head)}

    sources = (v_hbm, k_hbm, decay_hbm, beta_hbm, q_hbm, gain_hbm)
    targets = (v_ref, k_ref, decay_ref, beta_ref, q_ref, gain_ref)
    loads = [
        pltpu.make_async_copy(source, target, load_sem.at[at])
        for at, (source, target) in enumerate(zip(sources, targets))
    ]
    for load in loads:
        load.start()

    barrier = pltpu.get_barrier_semaphore()
    for step in range(1, n_head):
        pl.semaphore_signal(barrier, inc=1, device_id=partner(step), device_id_type=MESH)
    odd = lax.rem(seq, 2)
    mate = {"seq": seq + 1 - 2 * odd}
    for ahead in (2, n_seq - 2):
        pl.semaphore_signal(
            barrier, inc=1, device_id={"seq": lax.rem(seq + ahead, n_seq)}, device_id_type=MESH
        )
    pl.semaphore_signal(barrier, inc=1, device_id=mate, device_id_type=MESH)

    size = PACK * tokens
    row = lax.broadcasted_iota(jnp.int32, (size, size), 0)
    col = lax.broadcasted_iota(jnp.int32, (size, size), 1)

    def same(block):
        return (row // block) == (col // block)

    within = same(tokens) & (row >= col)
    strict = same(tokens) & (row > col)
    identity = jnp.where(row == col, 1.0, 0.0)
    first_head = lax.broadcasted_iota(jnp.int32, (1, size), 1) < tokens
    row_t = lax.broadcasted_iota(jnp.int32, (tokens, tokens), 0)
    col_t = lax.broadcasted_iota(jnp.int32, (tokens, tokens), 1)
    token_of = lax.rem(lax.broadcasted_iota(jnp.int32, (tokens, size), 1), tokens)
    before = lax.broadcasted_iota(jnp.int32, (tokens, size), 0) <= token_of
    lane = lax.broadcasted_iota(jnp.int32, (tokens, heads), 1)

    def stack(ref, ids):
        return jnp.concatenate([ref[pl.ds(i, tokens, stride=heads), :] for i in ids], axis=0)

    def held_rows(first_row, pack):
        kept_rows = []
        for step, part in pack:
            source = terms_in.at[me] if step == 0 else terms_out.at[step]
            kept_rows.append(source[first_row + part * tokens : first_row + (part + 1) * tokens, :])
        return jnp.concatenate(kept_rows, axis=0)

    def column(gate, i):
        picked = jnp.sum(jnp.where(lane == i, gate, 0.0), axis=1, keepdims=True)
        return jnp.broadcast_to(picked, (tokens, width))

    def batch_terms(packs):
        ids = [[lax.rem(me + step, n_head) * own + part for step, part in pack] for pack in packs]
        cums = [[column(cumulative, i) for i in pack] for pack in ids]
        cum = [jnp.concatenate(pack, axis=0) for pack in cums]
        beta = [jnp.concatenate([column(betas, i) for i in pack], axis=0) for pack in ids]
        across = [
            jnp.where(first_head, row_gate[pl.ds(pack[0], 1), :], row_gate[pl.ds(pack[1], 1), :])
            for pack in ids
        ]
        spread = [jnp.exp(jnp.where(within, c - a, -1e30)) for c, a in zip(cum, across)]
        keys = [held_rows(rows, pack) for pack in packs]
        lower = [
            jnp.where(strict, dot(k, k, NT) * s, 0.0) * b for k, s, b in zip(keys, spread, beta)
        ]
        block = 8
        inner = [jnp.where(same(block), a, 0.0) for a in lower]
        inner_short = short(inner)
        inverse = [identity - a for a in inner]
        square = short([dot(a, a) for a in inner_short])
        fourth = short([dot(a, a) for a in square])
        inverse = [x + dot(y, a) for x, y, a in zip(inverse, short(inverse), square)]
        inverse = [x + dot(y, a) for x, y, a in zip(inverse, short(inverse), fourth)]
        while block < tokens:
            between = same(2 * block) & ~same(block)
            corner = short([jnp.where(between, a, 0.0) for a in lower])
            held = short(inverse)
            crossed = short([dot(x, a) for x, a in zip(held, corner)])
            block *= 2
            if block < tokens:
                inverse = [x - dot(a, y) for x, a, y in zip(inverse, crossed, held)]
        scales = [
            jnp.where(first_head, beta_rows[pl.ds(pack[0], 1), :], beta_rows[pl.ds(pack[1], 1), :])
            for pack in ids
        ]
        solver = short([
            (x - dot(a, y)) * b for x, a, y, b in zip(inverse, crossed, held, scales)
        ])
        return [
            dict(units=pack, ids=i, spread=s, keys=k, cum=c, solver=t)
            for pack, i, s, k, c, t in zip(packs, ids, spread, keys, cum, solver)
        ]

    def terms_copy(step, what):
        section = (slice(0, rows), slice(rows, 2 * rows + 16))[what]
        return pltpu.make_async_remote_copy(
            src_ref=terms_out.at[step, section], dst_ref=terms_in.at[me, section],
            send_sem=terms_send.at[what, step], recv_sem=terms_recv.at[what, step],
            device_id=partner(step), device_id_type=MESH,
        )

    def query_copy(step):
        return pltpu.make_async_remote_copy(
            src_ref=query_out.at[step], dst_ref=query_in.at[me],
            send_sem=query_send.at[step], recv_sem=query_recv.at[step],
            device_id=partner(step), device_id_type=MESH,
        )

    def solver_copy(step):
        return pltpu.make_async_remote_copy(
            src_ref=solver_out.at[step], dst_ref=solver_in.at[me],
            send_sem=solver_send.at[step], recv_sem=solver_recv.at[step],
            device_id=partner(step), device_id_type=MESH,
        )

    tail_row = lax.broadcasted_iota(jnp.int32, (16, width), 0)

    def store_values(step):
        target = terms_in.at[me] if step == 0 else terms_out.at[step]
        for part in range(own):
            head, to = lax.rem(me + step, n_head) * own + part, part * tokens
            from_head = pl.ds(head, tokens, stride=heads)
            target[to : to + tokens, :] = v_rows[from_head, :].astype(BF16)
        if step:
            terms_copy(step, 0).start()

    def store_keys(step):
        target = terms_in.at[me] if step == 0 else terms_out.at[step]
        tail = jnp.zeros((16, width), F32)
        for part in range(own):
            head, to = lax.rem(me + step, n_head) * own + part, part * tokens
            from_head = pl.ds(head, tokens, stride=heads)
            target[rows + to : rows + to + tokens, :] = k_rows[from_head, :].astype(BF16)
            decay = kept_gate[1, pl.ds(head, 1), :]
            high = decay.astype(BF16).astype(F32)
            tail = jnp.where(tail_row == 3 * part, kept_gate[0, pl.ds(head, 1), :], tail)
            tail = jnp.where(tail_row == 3 * part + 1, high, tail)
            tail = jnp.where(tail_row == 3 * part + 2, decay - high, tail)
        target[2 * rows :, :] = tail.astype(BF16)
        if step:
            terms_copy(step, 1).start()

    pairs = max(own // 2, 1)

    def store_solvers(batch):
        for data in batch:
            scaled = data["solver"]
            top, low = scaled[:tokens], scaled[tokens:]
            for at, (step, part) in enumerate(data["units"]):
                target = solver_in.at[me] if step == 0 else solver_out.at[step]
                if own == 1:
                    mine = (top, low)[at]
                    both = jnp.concatenate([mine[:, tokens:], mine[:, :tokens]], axis=1) + mine
                    target[...] = both
                elif at == 0:
                    to = part // 2 * tokens
                    target[to : to + tokens, :] = top + low

    def score_terms(batch):
        queries = [stack(q_rows, data["ids"]).astype(BF16) for data in batch]
        scores = short([dot(q, d["keys"], NT) * d["spread"] for q, d in zip(queries, batch)])
        grown = [jnp.exp(d["cum"]) for d in batch]
        right = [
            jnp.concatenate(
                [held_rows(0, d["units"]), (d["keys"].astype(F32) * g).astype(BF16)],
                axis=1,
            )
            for d, g in zip(batch, grown)
        ]
        solved = short([dot(d["solver"], r) for d, r in zip(batch, right)])
        return [
            dict(units=d["units"], gated=q.astype(F32) * g, scores=c, solved=x)
            for d, q, g, c, x in zip(batch, queries, grown, scores, solved)
        ]

    def query_terms(batch):
        mixed = [dot(d["scores"], d["solved"]) for d in batch]
        for m, d in zip(mixed, batch):
            through = (d["gated"] - m[:, width:]).astype(BF16)
            for at, (step, part) in enumerate(d["units"]):
                section, to = slice(at * tokens, (at + 1) * tokens), part * tokens
                target = query_in.at[me] if step == 0 else query_out.at[step]
                target[to : to + tokens, :] = through[section]
                offset[step, part] = m[section, :width]

    order = list(range(1, n_head)) + [0]
    units = [(step, part) for step in order for part in range(own)]
    packs = [units[at : at + PACK] for at in range(0, len(units), PACK)]
    loads[0].wait()
    v_rows[...] = v_ref[...].astype(F32).reshape(-1, width)
    pl.semaphore_wait(barrier, n_head + 2)
    for step in order:
        store_values(step)
    loads[2].wait()
    log_rows = dot(decay_ref[...], jnp.where(before, 1.0, 0.0).astype(BF16))
    row_gate[...] = log_rows
    log_end = log_rows[:, size - 1 :]
    first_half = lax.broadcasted_iota(jnp.int32, (heads, size), 1) < tokens
    kept_gate[0] = jnp.exp(jnp.where(first_half, log_rows, log_end - log_rows))
    kept_gate[1] = jnp.broadcast_to(jnp.exp(log_end), (heads, size))
    cumulative = dot(jnp.where(row_t >= col_t, 1.0, 0.0).astype(BF16), decay_ref[...], NT)
    loads[3].wait()
    row_beta = dot(beta_ref[...], jnp.where(token_of == lax.broadcasted_iota(
        jnp.int32, (tokens, size), 0), 1.0, 0.0).astype(BF16))
    beta_rows[...] = row_beta
    betas = dot(jnp.where(row_t == col_t, 1.0, 0.0).astype(BF16), beta_ref[...], NT)
    loads[1].wait()
    k_rows[...] = unit(k_ref[...])
    for step in order:
        store_keys(step)
    kept = []
    for at in range(0, len(packs), BATCH):
        batch = batch_terms(packs[at : at + BATCH])
        store_solvers(batch)
        kept.append(batch)
    for step in range(1, n_head):
        solver_copy(step).start()
    loads[4].wait()
    q_rows[...] = unit(q_ref[...]) * width ** (-0.5)
    loads[5].wait()
    scored = [score_terms(batch) for batch in kept]
    for batch in scored:
        query_terms(batch)
    for step in range(1, n_head):
        query_copy(step).start()

    for step in range(1, n_head):
        terms_copy(step, 0).wait_recv()
        terms_copy(step, 1).wait_recv()
    low_lane = lax.broadcasted_iota(jnp.int32, (tokens, size), 1) < tokens
    eye_t = row_t == col_t
    shrunk = []
    for group in range(n_head):
        tail = terms_in[group, 2 * rows :, :].astype(F32)
        for part in range(own):
            keys = terms_in[group, rows + part * tokens : rows + (part + 1) * tokens, :]
            shrink = tail[3 * part : 3 * part + 1, tokens:]
            shrunk.append(dot(jnp.where(eye_t, shrink, 0.0).astype(BF16), keys).astype(BF16))
    for step in range(1, n_head):
        solver_copy(step).wait_recv()
    erasers_of, pseudo_of = [], []
    for group in range(n_head):
        tail = terms_in[group, 2 * rows :, :].astype(F32)
        for pair in range(pairs):
            solver = solver_in[group, pair * tokens : (pair + 1) * tokens, :].astype(F32)
            many = min(own, 2)
            grows = [tail[3 * part : 3 * part + 1, :] for part in range(many * pair, many * pair + many)]
            if many == 2:
                mirrored = jnp.concatenate([grows[1][:, tokens:], grows[1][:, :tokens]], axis=1)
                grow = jnp.where(first_head, grows[0], mirrored)
                diagonal = lambda t: jnp.concatenate(
                    [jnp.where(low_lane, t, 0.0), jnp.where(low_lane, 0.0, t)], axis=0
                ).astype(BF16)
            else:
                grow = grows[0]
                diagonal = lambda t: t[:, :tokens].astype(BF16)
            section = slice(pair * many * tokens, (pair + 1) * many * tokens)
            beyond = slice(rows + section.start, rows + section.stop)
            erasers = dot(diagonal(solver * grow), terms_in[group, beyond, :]).astype(BF16)
            pseudo = dot(diagonal(solver), terms_in[group, section, :]).astype(BF16)
            for at in range(many):
                erasers_of.append(erasers[at * tokens : (at + 1) * tokens])
                pseudo_of.append(pseudo[at * tokens : (at + 1) * tokens])
    eye = jnp.where(
        lax.broadcasted_iota(jnp.int32, (width, width), 0)
        == lax.broadcasted_iota(jnp.int32, (width, width), 1), 1.0, 0.0,
    )
    current = [jnp.concatenate([eye, jnp.zeros((width, width), F32)], axis=1)] * own
    for group in range(n_head):
        tail = terms_in[group, 2 * rows :, :].astype(F32)
        held = short(current)
        for part in range(own):
            prefix[part, group] = held[part]
        for part in range(own):
            pseudo = pseudo_of[group * own + part]
            erasers = erasers_of[group * own + part]
            carried = shrunk[group * own + part]
            decay = tail[3 * part + 1 : 3 * part + 2, :] + tail[3 * part + 2 : 3 * part + 3, :]
            if group:
                erased = dot(erasers, held[part])
                change = jnp.concatenate(
                    [erased[:, :width], erased[:, width:] - pseudo.astype(F32)], axis=1
                ).astype(BF16)
            else:
                change = jnp.concatenate([erasers, -pseudo], axis=1)
            decay = jnp.concatenate([decay, decay], axis=1)
            current[part] = current[part] * decay - dot(carried, change, TN)
    def map_copy(part, what):
        section = (slice(0, 2), slice(2, 3))[what]
        return pltpu.make_async_remote_copy(
            src_ref=slab_map.at[part, section], dst_ref=front_map.at[part, section],
            send_sem=map_send.at[what, part], recv_sem=map_recv.at[what, part],
            device_id=mate, device_id_type=MESH,
        )

    def entry_copy(part):
        return pltpu.make_async_remote_copy(
            src_ref=chain_in.at[part], dst_ref=entry.at[part],
            send_sem=entry_send.at[part], recv_sem=entry_recv.at[part],
            device_id=mate, device_id_type=MESH,
        )

    def chain_copy(part):
        return pltpu.make_async_remote_copy(
            src_ref=chain_out.at[part], dst_ref=chain_in.at[part],
            send_sem=chain_send.at[part], recv_sem=chain_recv.at[part],
            device_id={"seq": lax.rem(seq + 2, n_seq)}, device_id_type=MESH,
        )

    def keep(target, part, linear):
        high = linear.astype(BF16)
        target[part, 0] = high
        target[part, 1] = (linear - high.astype(F32)).astype(BF16)

    for part in range(own):
        keep(slab_map, part, current[part][:, :width])
        slab_map[part, 2] = current[part][:, width:].astype(BF16)
        slab_add[part] = current[part][:, width:]

    first, last, late = seq < 2, seq >= n_seq - 2, seq >= n_seq // 2

    @pl.when(odd == 0)
    def _():
        for part in range(own):
            map_copy(part, 1).start()

        @pl.when(jnp.logical_not(first))
        def _():
            for part in range(own):
                map_copy(part, 0).start()

    def core_copy(step, part):
        slot = n_head - step
        group = lax.rem(me + step, n_head)
        return pltpu.make_async_remote_copy(
            src_ref=core_out.at[part, group], dst_ref=core_in.at[slot, part],
            send_sem=core_send.at[step, part], recv_sem=core_recv.at[slot, part],
            device_id=partner(step), device_id_type=MESH,
        )

    def map_queries():
        for step in range(1, n_head):
            query_copy(step).wait_recv()
        for group in range(n_head):
            for part in range(own):
                section = slice(group * tokens, (group + 1) * tokens)
                at = part * tokens
                queries = query_in[group, at : at + tokens, :]
                mapped = dot(queries, prefix[part, group])
                query_map[part, section, :] = mapped[:, :width].astype(BF16)
                query_add[part, section, :] = mapped[:, width:]

    def give_cores(part):
        cores = dot(query_map[part], entry[part]) + query_add[part]
        core_out[part] = cores.astype(BF16).reshape(n_head, tokens, width)
        for step in range(1, n_head):
            core_copy(step, part).start()

    def send_on(part):
        @pl.when(jnp.logical_not(last))
        def _():
            chain_copy(part).start()

    def compose_chip():
        for part in range(own):
            map_copy(part, 1).wait_recv()
            map_copy(part, 0).wait_recv()
            high, low = slab_map[part, 0], slab_map[part, 1]
            front, front_low, front_add = (front_map[part, at] for at in range(3))
            linear = dot(high, front) + (dot(low, front) + dot(high, front_low))
            keep(chip_map, part, linear)
            chip_add[part] = dot(high, front_add) + dot(low, front_add) + slab_add[part]

    def pass_on(part):
        chain_copy(part).wait_recv()

        @pl.when(jnp.logical_not(last))
        def _():
            state = chain_in[part]
            moved = dot(chip_map[part, 0], state) + dot(chip_map[part, 1], state)
            chain_out[part] = (moved + chip_add[part]).astype(BF16)
            chain_copy(part).start()

        entry_copy(part).start()

    def enter(part):
        state = chain_in[part]
        moved = dot(front_map[part, 0], state) + dot(front_map[part, 1], state)
        entry[part] = (moved + front_map[part, 2].astype(F32)).astype(BF16)
        give_cores(part)

    @pl.when(odd == 0)
    def _():
        map_queries()

        @pl.when(first)
        def _():
            entry[...] = jnp.zeros_like(entry)

        for part in range(own):
            @pl.when(jnp.logical_not(first))
            def _():
                entry_copy(part).wait_recv()

            give_cores(part)
        for part in range(own):
            map_copy(part, 1).wait_send()

            @pl.when(jnp.logical_not(first))
            def _():
                map_copy(part, 0).wait_send()

    @pl.when((odd == 1) & first)
    def _():
        for part in range(own):
            map_copy(part, 1).wait_recv()
            state = front_map[part, 2]
            entry[part] = state
            moved = dot(slab_map[part, 0], state) + dot(slab_map[part, 1], state)
            chain_out[part] = (moved + slab_add[part]).astype(BF16)
            send_on(part)
        map_queries()
        for part in range(own):
            give_cores(part)

    @pl.when((odd == 1) & jnp.logical_not(first))
    def _():
        compose_chip()

        @pl.when(last)
        def _():
            map_queries()
            for part in range(own):
                pass_on(part)
                if part:
                    enter(part - 1)
            enter(own - 1)

        @pl.when(jnp.logical_not(last))
        def _():
            @pl.when(late)
            def _():
                map_queries()

            for part in range(own):
                pass_on(part)

            @pl.when(jnp.logical_not(late))
            def _():
                map_queries()

            for part in range(own):
                enter(part)

        for part in range(own):
            entry_copy(part).wait_send()

    @pl.when((odd == 1) & jnp.logical_not(last))
    def _():
        for part in range(own):
            chain_copy(part).wait_send()

    gain = gain_ref[...]
    for step in [0] + list(range(n_head - 1, 0, -1)):
        for part in range(own):
            if step:
                core_copy(n_head - step, part).wait_recv()
                core = core_in[step, part]
            else:
                core = core_out[part, me]
            core = core.astype(F32) + offset[step, part]
            scale = lax.rsqrt(jnp.mean(core * core, axis=-1, keepdims=True) + 1e-06)
            head = lax.rem(me + step, n_head) * own + part
            out_rows[pl.ds(head, tokens, stride=heads), :] = core * scale * gain
    out_ref[...] = out_rows[...].reshape(tokens, heads, width).astype(BF16)

    for step in range(1, n_head):
        terms_copy(step, 0).wait_send()
        terms_copy(step, 1).wait_send()
        solver_copy(step).wait_send()
        query_copy(step).wait_send()
        for part in range(own):
            core_copy(step, part).wait_send()


def solution(mesh):
    n_seq, n_head = mesh.shape["seq"], mesh.shape["head"]

    def local(queries, keys, values, log_decay, beta, norm_gain):
        tokens, heads, width = queries.shape
        own = heads // n_head
        length = tokens * heads
        hbm = pl.BlockSpec(memory_space=pltpu.HBM)
        payload = (n_head, 2 * own * tokens + 16, width)
        solvers = (n_head, max(own // 2, 1) * tokens, 2 * tokens)
        dma = pltpu.SemaphoreType.DMA
        return pl.pallas_call(
            functools.partial(kernel, n_seq, n_head),
            out_shape=pltpu.VMEM(queries.shape, BF16),
            in_specs=[hbm] * 6,
            out_specs=pl.BlockSpec(memory_space=pltpu.VMEM),
            scratch_shapes=[
                pltpu.VMEM(queries.shape, BF16),
                pltpu.VMEM(queries.shape, BF16),
                pltpu.VMEM(queries.shape, BF16),
                pltpu.VMEM((heads, tokens), BF16),
                pltpu.VMEM((heads, tokens), BF16),
                pltpu.VMEM((1, width), F32),
                pltpu.VMEM((length, width), F32),
                pltpu.VMEM((length, width), F32),
                pltpu.VMEM((length, width), F32),
                pltpu.VMEM((length, width), F32),
                pltpu.VMEM((heads, PACK * tokens), F32),
                pltpu.VMEM((heads, PACK * tokens), F32),
                pltpu.VMEM((2, heads, PACK * tokens), F32),
                pltpu.VMEM(payload, BF16),
                pltpu.VMEM(payload, BF16),
                pltpu.VMEM(solvers, BF16),
                pltpu.VMEM(solvers, BF16),
                pltpu.VMEM((n_head, own * tokens, width), BF16),
                pltpu.VMEM((n_head, own * tokens, width), BF16),
                pltpu.VMEM((n_head, own, tokens, width), F32),
                pltpu.VMEM((own, n_head, width, 2 * width), BF16),
                pltpu.VMEM((own, 3, width, width), BF16),
                pltpu.VMEM((own, width, width), F32),
                pltpu.VMEM((own, 3, width, width), BF16),
                pltpu.VMEM((own, 2, width, width), BF16),
                pltpu.VMEM((own, width, width), F32),
                pltpu.VMEM((own, width, width), BF16),
                pltpu.VMEM((own, n_head * tokens, width), BF16),
                pltpu.VMEM((own, n_head * tokens, width), F32),
                pltpu.VMEM((own, width, width), BF16),
                pltpu.VMEM((own, width, width), BF16),
                pltpu.VMEM((own, n_head, tokens, width), BF16),
                pltpu.VMEM((n_head, own, tokens, width), BF16),
                dma((6,)),
                dma((2, n_head)),
                dma((2, n_head)),
                dma((n_head,)),
                dma((n_head,)),
                dma((n_head,)),
                dma((n_head,)),
                dma((2, own)),
                dma((2, own)),
                dma((own,)),
                dma((own,)),
                dma((own,)),
                dma((own,)),
                dma((n_head, own)),
                dma((n_head, own)),
            ],
            compiler_params=pltpu.CompilerParams(
                collective_id=0, has_side_effects=True, vmem_limit_bytes=48 * 1024 * 1024
            ),
            name="gated_delta",
        )(*[
            pltpu.with_memory_space_constraint(array, pltpu.HBM)
            for array in (queries, keys, values, log_decay.T, beta.T, norm_gain.reshape(1, width))
        ])

    tokens_by_device = P(("seq", "head"), None, None)
    placed = (tokens_by_device,) * 3 + (P(("seq", "head"), None),) * 2 + (P(),)
    return jax.shard_map(
        local, mesh=mesh, in_specs=placed, out_specs=tokens_by_device, check_vma=False
    )
```

```python
import functools

import jax
import jax.numpy as jnp
from jax import lax
from jax.experimental import pallas as pl
from jax.experimental.pallas import tpu as pltpu
from jax.sharding import PartitionSpec as P

PACK = 2
BATCH = 8
MESH = pl.DeviceIdType.MESH
F32, BF16 = jnp.float32, jnp.bfloat16
NT, TN = ((1,), (1,)), ((0,), (0,))


def dot(left, right, dims=((1,), (0,))):
    return lax.dot_general(left, right, (dims, ((), ())), preferred_element_type=F32)


def short(tensors):
    return [tensor.astype(BF16) for tensor in tensors]


def unit(tensor):
    flat = tensor.astype(F32).reshape(-1, tensor.shape[-1])
    return flat * lax.rsqrt(jnp.sum(flat * flat, axis=-1, keepdims=True) + 1e-06)


def kernel(
    n_seq, n_head, q_hbm, k_hbm, v_hbm, decay_hbm, beta_hbm, gain_hbm, out_ref,
    q_ref, k_ref, v_ref, decay_ref, beta_ref, gain_ref,
    q_rows, k_rows, v_rows, out_rows, row_gate, beta_rows, kept_gate, terms_out, terms_in, solver_out, solver_in, query_out, query_in, offset,
    prefix, slab_map, slab_add, front_map, chip_map, chip_add, entry, query_map, query_add,
    chain_in, chain_out, core_out, core_in,
    load_sem, terms_send, terms_recv, solver_send, solver_recv, query_send, query_recv,
    map_send, map_recv, entry_send, entry_recv, chain_send, chain_recv, core_send, core_recv,
):
    seq, me = lax.axis_index("seq"), lax.axis_index("head")
    tokens, heads, width = q_ref.shape
    own = heads // n_head
    rows = own * tokens

    def partner(step):
        return {"head": lax.rem(me + step, n_head)}

    sources = (v_hbm, k_hbm, decay_hbm, beta_hbm, q_hbm, gain_hbm)
    targets = (v_ref, k_ref, decay_ref, beta_ref, q_ref, gain_ref)
    loads = [
        pltpu.make_async_copy(source, target, load_sem.at[at])
        for at, (source, target) in enumerate(zip(sources, targets))
    ]
    for load in loads:
        load.start()

    barrier = pltpu.get_barrier_semaphore()
    for step in range(1, n_head):
        pl.semaphore_signal(barrier, inc=1, device_id=partner(step), device_id_type=MESH)
    odd = lax.rem(seq, 2)
    mate = {"seq": seq + 1 - 2 * odd}
    for ahead in (2, n_seq - 2):
        pl.semaphore_signal(
            barrier, inc=1, device_id={"seq": lax.rem(seq + ahead, n_seq)}, device_id_type=MESH
        )
    pl.semaphore_signal(barrier, inc=1, device_id=mate, device_id_type=MESH)

    size = PACK * tokens
    row = lax.broadcasted_iota(jnp.int32, (size, size), 0)
    col = lax.broadcasted_iota(jnp.int32, (size, size), 1)

    def same(block):
        return (row // block) == (col // block)

    within = same(tokens) & (row >= col)
    strict = same(tokens) & (row > col)
    identity = jnp.where(row == col, 1.0, 0.0)
    first_head = lax.broadcasted_iota(jnp.int32, (1, size), 1) < tokens
    row_t = lax.broadcasted_iota(jnp.int32, (tokens, tokens), 0)
    col_t = lax.broadcasted_iota(jnp.int32, (tokens, tokens), 1)
    token_of = lax.rem(lax.broadcasted_iota(jnp.int32, (tokens, size), 1), tokens)
    before = lax.broadcasted_iota(jnp.int32, (tokens, size), 0) <= token_of
    lane = lax.broadcasted_iota(jnp.int32, (tokens, heads), 1)

    def stack(ref, ids):
        return jnp.concatenate([ref[pl.ds(i, tokens, stride=heads), :] for i in ids], axis=0)

    def held_rows(first_row, pack):
        kept_rows = []
        for step, part in pack:
            source = terms_in.at[me] if step == 0 else terms_out.at[step]
            kept_rows.append(source[first_row + part * tokens : first_row + (part + 1) * tokens, :])
        return jnp.concatenate(kept_rows, axis=0)

    def column(gate, i):
        picked = jnp.sum(jnp.where(lane == i, gate, 0.0), axis=1, keepdims=True)
        return jnp.broadcast_to(picked, (tokens, width))

    def batch_terms(packs):
        ids = [[lax.rem(me + step, n_head) * own + part for step, part in pack] for pack in packs]
        cums = [[column(cumulative, i) for i in pack] for pack in ids]
        cum = [jnp.concatenate(pack, axis=0) for pack in cums]
        beta = [jnp.concatenate([column(betas, i) for i in pack], axis=0) for pack in ids]
        across = [
            jnp.where(first_head, row_gate[pl.ds(pack[0], 1), :], row_gate[pl.ds(pack[1], 1), :])
            for pack in ids
        ]
        spread = [jnp.exp(jnp.where(within, c - a, -1e30)) for c, a in zip(cum, across)]
        keys = [held_rows(rows, pack) for pack in packs]
        lower = [
            jnp.where(strict, dot(k, k, NT) * s, 0.0) * b for k, s, b in zip(keys, spread, beta)
        ]
        block = 8
        inner = [jnp.where(same(block), a, 0.0) for a in lower]
        inner_short = short(inner)
        inverse = [identity - a for a in inner]
        square = short([dot(a, a) for a in inner_short])
        fourth = short([dot(a, a) for a in square])
        inverse = [x + dot(y, a) for x, y, a in zip(inverse, short(inverse), square)]
        inverse = [x + dot(y, a) for x, y, a in zip(inverse, short(inverse), fourth)]
        while block < tokens:
            between = same(2 * block) & ~same(block)
            corner = short([jnp.where(between, a, 0.0) for a in lower])
            held = short(inverse)
            crossed = short([dot(x, a) for x, a in zip(held, corner)])
            block *= 2
            if block < tokens:
                inverse = [x - dot(a, y) for x, a, y in zip(inverse, crossed, held)]
        scales = [
            jnp.where(first_head, beta_rows[pl.ds(pack[0], 1), :], beta_rows[pl.ds(pack[1], 1), :])
            for pack in ids
        ]
        solver = short([
            (x - dot(a, y)) * b for x, a, y, b in zip(inverse, crossed, held, scales)
        ])
        return [
            dict(units=pack, ids=i, spread=s, keys=k, cum=c, solver=t)
            for pack, i, s, k, c, t in zip(packs, ids, spread, keys, cum, solver)
        ]

    def terms_copy(step, what):
        section = (slice(0, rows), slice(rows, 2 * rows + 16))[what]
        return pltpu.make_async_remote_copy(
            src_ref=terms_out.at[step, section], dst_ref=terms_in.at[me, section],
            send_sem=terms_send.at[what, step], recv_sem=terms_recv.at[what, step],
            device_id=partner(step), device_id_type=MESH,
        )

    def query_copy(step):
        return pltpu.make_async_remote_copy(
            src_ref=query_out.at[step], dst_ref=query_in.at[me],
            send_sem=query_send.at[step], recv_sem=query_recv.at[step],
            device_id=partner(step), device_id_type=MESH,
        )

    def solver_copy(step):
        return pltpu.make_async_remote_copy(
            src_ref=solver_out.at[step], dst_ref=solver_in.at[me],
            send_sem=solver_send.at[step], recv_sem=solver_recv.at[step],
            device_id=partner(step), device_id_type=MESH,
        )

    tail_row = lax.broadcasted_iota(jnp.int32, (16, width), 0)

    def store_values(step):
        target = terms_in.at[me] if step == 0 else terms_out.at[step]
        for part in range(own):
            head, to = lax.rem(me + step, n_head) * own + part, part * tokens
            from_head = pl.ds(head, tokens, stride=heads)
            target[to : to + tokens, :] = v_rows[from_head, :].astype(BF16)
        if step:
            terms_copy(step, 0).start()

    def store_keys(step):
        target = terms_in.at[me] if step == 0 else terms_out.at[step]
        tail = jnp.zeros((16, width), F32)
        for part in range(own):
            head, to = lax.rem(me + step, n_head) * own + part, part * tokens
            from_head = pl.ds(head, tokens, stride=heads)
            target[rows + to : rows + to + tokens, :] = k_rows[from_head, :].astype(BF16)
            decay = kept_gate[1, pl.ds(head, 1), :]
            high = decay.astype(BF16).astype(F32)
            tail = jnp.where(tail_row == 3 * part, kept_gate[0, pl.ds(head, 1), :], tail)
            tail = jnp.where(tail_row == 3 * part + 1, high, tail)
            tail = jnp.where(tail_row == 3 * part + 2, decay - high, tail)
        target[2 * rows :, :] = tail.astype(BF16)
        if step:
            terms_copy(step, 1).start()

    pairs = max(own // 2, 1)

    def store_solvers(batch):
        for data in batch:
            scaled = data["solver"]
            top, low = scaled[:tokens], scaled[tokens:]
            for at, (step, part) in enumerate(data["units"]):
                target = solver_in.at[me] if step == 0 else solver_out.at[step]
                if own == 1:
                    mine = (top, low)[at]
                    both = jnp.concatenate([mine[:, tokens:], mine[:, :tokens]], axis=1) + mine
                    target[...] = both
                elif at == 0:
                    to = part // 2 * tokens
                    target[to : to + tokens, :] = top + low

    def score_terms(batch):
        queries = [stack(q_rows, data["ids"]).astype(BF16) for data in batch]
        scores = short([dot(q, d["keys"], NT) * d["spread"] for q, d in zip(queries, batch)])
        grown = [jnp.exp(d["cum"]) for d in batch]
        right = [
            jnp.concatenate(
                [held_rows(0, d["units"]), (d["keys"].astype(F32) * g).astype(BF16)],
                axis=1,
            )
            for d, g in zip(batch, grown)
        ]
        solved = short([dot(d["solver"], r) for d, r in zip(batch, right)])
        return [
            dict(units=d["units"], gated=q.astype(F32) * g, scores=c, solved=x)
            for d, q, g, c, x in zip(batch, queries, grown, scores, solved)
        ]

    def query_terms(batch):
        mixed = [dot(d["scores"], d["solved"]) for d in batch]
        for m, d in zip(mixed, batch):
            through = (d["gated"] - m[:, width:]).astype(BF16)
            for at, (step, part) in enumerate(d["units"]):
                section, to = slice(at * tokens, (at + 1) * tokens), part * tokens
                target = query_in.at[me] if step == 0 else query_out.at[step]
                target[to : to + tokens, :] = through[section]
                offset[step, part] = m[section, :width]

    order = list(range(1, n_head)) + [0]
    units = [(step, part) for step in order for part in range(own)]
    packs = [units[at : at + PACK] for at in range(0, len(units), PACK)]
    loads[0].wait()
    v_rows[...] = v_ref[...].astype(F32).reshape(-1, width)
    pl.semaphore_wait(barrier, n_head + 2)
    for step in order:
        store_values(step)
    loads[2].wait()
    log_rows = dot(decay_ref[...], jnp.where(before, 1.0, 0.0).astype(BF16))
    row_gate[...] = log_rows
    log_end = log_rows[:, size - 1 :]
    first_half = lax.broadcasted_iota(jnp.int32, (heads, size), 1) < tokens
    kept_gate[0] = jnp.exp(jnp.where(first_half, log_rows, log_end - log_rows))
    kept_gate[1] = jnp.broadcast_to(jnp.exp(log_end), (heads, size))
    cumulative = dot(jnp.where(row_t >= col_t, 1.0, 0.0).astype(BF16), decay_ref[...], NT)
    loads[3].wait()
    row_beta = dot(beta_ref[...], jnp.where(token_of == lax.broadcasted_iota(
        jnp.int32, (tokens, size), 0), 1.0, 0.0).astype(BF16))
    beta_rows[...] = row_beta
    betas = dot(jnp.where(row_t == col_t, 1.0, 0.0).astype(BF16), beta_ref[...], NT)
    loads[1].wait()
    k_rows[...] = unit(k_ref[...])
    for step in order:
        store_keys(step)
    kept = []
    for at in range(0, len(packs), BATCH):
        batch = batch_terms(packs[at : at + BATCH])
        store_solvers(batch)
        kept.append(batch)
    for step in range(1, n_head):
        solver_copy(step).start()

    for step in range(1, n_head):
        terms_copy(step, 0).wait_recv()
        terms_copy(step, 1).wait_recv()
    low_lane = lax.broadcasted_iota(jnp.int32, (tokens, size), 1) < tokens
    eye_t = row_t == col_t
    shrunk = []
    for group in range(n_head):
        tail = terms_in[group, 2 * rows :, :].astype(F32)
        for part in range(own):
            keys = terms_in[group, rows + part * tokens : rows + (part + 1) * tokens, :]
            shrink = tail[3 * part : 3 * part + 1, tokens:]
            shrunk.append(dot(jnp.where(eye_t, shrink, 0.0).astype(BF16), keys).astype(BF16))
    for step in range(1, n_head):
        solver_copy(step).wait_recv()
    erasers_of, pseudo_of = [], []
    for group in range(n_head):
        tail = terms_in[group, 2 * rows :, :].astype(F32)
        for pair in range(pairs):
            solver = solver_in[group, pair * tokens : (pair + 1) * tokens, :].astype(F32)
            many = min(own, 2)
            grows = [tail[3 * part : 3 * part + 1, :] for part in range(many * pair, many * pair + many)]
            if many == 2:
                mirrored = jnp.concatenate([grows[1][:, tokens:], grows[1][:, :tokens]], axis=1)
                grow = jnp.where(first_head, grows[0], mirrored)
                diagonal = lambda t: jnp.concatenate(
                    [jnp.where(low_lane, t, 0.0), jnp.where(low_lane, 0.0, t)], axis=0
                ).astype(BF16)
            else:
                grow = grows[0]
                diagonal = lambda t: t[:, :tokens].astype(BF16)
            section = slice(pair * many * tokens, (pair + 1) * many * tokens)
            beyond = slice(rows + section.start, rows + section.stop)
            erasers = dot(diagonal(solver * grow), terms_in[group, beyond, :]).astype(BF16)
            pseudo = dot(diagonal(solver), terms_in[group, section, :]).astype(BF16)
            for at in range(many):
                erasers_of.append(erasers[at * tokens : (at + 1) * tokens])
                pseudo_of.append(pseudo[at * tokens : (at + 1) * tokens])
    eye = jnp.where(
        lax.broadcasted_iota(jnp.int32, (width, width), 0)
        == lax.broadcasted_iota(jnp.int32, (width, width), 1), 1.0, 0.0,
    )
    current = [jnp.concatenate([eye, jnp.zeros((width, width), F32)], axis=1)] * own
    for group in range(n_head):
        tail = terms_in[group, 2 * rows :, :].astype(F32)
        held = short(current)
        for part in range(own):
            prefix[part, group] = held[part]
        for part in range(own):
            pseudo = pseudo_of[group * own + part]
            erasers = erasers_of[group * own + part]
            carried = shrunk[group * own + part]
            decay = tail[3 * part + 1 : 3 * part + 2, :] + tail[3 * part + 2 : 3 * part + 3, :]
            if group:
                erased = dot(erasers, held[part])
                change = jnp.concatenate(
                    [erased[:, :width], erased[:, width:] - pseudo.astype(F32)], axis=1
                ).astype(BF16)
            else:
                change = jnp.concatenate([erasers, -pseudo], axis=1)
            decay = jnp.concatenate([decay, decay], axis=1)
            current[part] = current[part] * decay - dot(carried, change, TN)
    def map_copy(part, what):
        section = (slice(0, 2), slice(2, 3))[what]
        return pltpu.make_async_remote_copy(
            src_ref=slab_map.at[part, section], dst_ref=front_map.at[part, section],
            send_sem=map_send.at[what, part], recv_sem=map_recv.at[what, part],
            device_id=mate, device_id_type=MESH,
        )

    def entry_copy(part):
        return pltpu.make_async_remote_copy(
            src_ref=chain_in.at[part], dst_ref=entry.at[part],
            send_sem=entry_send.at[part], recv_sem=entry_recv.at[part],
            device_id=mate, device_id_type=MESH,
        )

    def chain_copy(part):
        return pltpu.make_async_remote_copy(
            src_ref=chain_out.at[part], dst_ref=chain_in.at[part],
            send_sem=chain_send.at[part], recv_sem=chain_recv.at[part],
            device_id={"seq": lax.rem(seq + 2, n_seq)}, device_id_type=MESH,
        )

    def keep(target, part, linear):
        high = linear.astype(BF16)
        target[part, 0] = high
        target[part, 1] = (linear - high.astype(F32)).astype(BF16)

    for part in range(own):
        keep(slab_map, part, current[part][:, :width])
        slab_map[part, 2] = current[part][:, width:].astype(BF16)
        slab_add[part] = current[part][:, width:]

    first, last, late = seq < 2, seq >= n_seq - 2, seq >= n_seq // 2

    def hand_over():
        for part in range(own):
            map_copy(part, 1).start()

        @pl.when(jnp.logical_not(first))
        def _():
            for part in range(own):
                map_copy(part, 0).start()

    @pl.when((odd == 0) & jnp.logical_not(late))
    def _():
        hand_over()

    @pl.when((odd == 1) & first)
    def _():
        for part in range(own):
            map_copy(part, 1).wait_recv()
            state = front_map[part, 2]
            entry[part] = state
            moved = dot(slab_map[part, 0], state) + dot(slab_map[part, 1], state)
            chain_out[part] = (moved + slab_add[part]).astype(BF16)

            @pl.when(jnp.logical_not(last))
            def _():
                chain_copy(part).start()

    loads[4].wait()
    q_rows[...] = unit(q_ref[...]) * width ** (-0.5)
    loads[5].wait()
    scored = [score_terms(batch) for batch in kept]
    for batch in scored:
        query_terms(batch)
    for step in range(1, n_head):
        query_copy(step).start()

    @pl.when((odd == 0) & late)
    def _():
        hand_over()

    def core_copy(step, part):
        slot = n_head - step
        group = lax.rem(me + step, n_head)
        return pltpu.make_async_remote_copy(
            src_ref=core_out.at[part, group], dst_ref=core_in.at[slot, part],
            send_sem=core_send.at[step, part], recv_sem=core_recv.at[slot, part],
            device_id=partner(step), device_id_type=MESH,
        )

    def map_queries():
        for step in range(1, n_head):
            query_copy(step).wait_recv()
        for group in range(n_head):
            for part in range(own):
                section = slice(group * tokens, (group + 1) * tokens)
                at = part * tokens
                queries = query_in[group, at : at + tokens, :]
                mapped = dot(queries, prefix[part, group])
                query_map[part, section, :] = mapped[:, :width].astype(BF16)
                query_add[part, section, :] = mapped[:, width:]

    def give_cores(part):
        cores = dot(query_map[part], entry[part]) + query_add[part]
        core_out[part] = cores.astype(BF16).reshape(n_head, tokens, width)
        for step in range(1, n_head):
            core_copy(step, part).start()

    def compose_chip():
        for part in range(own):
            map_copy(part, 1).wait_recv()
            map_copy(part, 0).wait_recv()
            high, low = slab_map[part, 0], slab_map[part, 1]
            front, front_low, front_add = (front_map[part, at] for at in range(3))
            linear = dot(high, front) + (dot(low, front) + dot(high, front_low))
            keep(chip_map, part, linear)
            chip_add[part] = dot(high, front_add) + dot(low, front_add) + slab_add[part]

    def pass_on(part):
        chain_copy(part).wait_recv()

        @pl.when(jnp.logical_not(last))
        def _():
            state = chain_in[part]
            moved = dot(chip_map[part, 0], state) + dot(chip_map[part, 1], state)
            chain_out[part] = (moved + chip_add[part]).astype(BF16)
            chain_copy(part).start()

        entry_copy(part).start()

    def enter(part):
        state = chain_in[part]
        moved = dot(front_map[part, 0], state) + dot(front_map[part, 1], state)
        entry[part] = (moved + front_map[part, 2].astype(F32)).astype(BF16)
        give_cores(part)

    @pl.when(odd == 0)
    def _():
        map_queries()

        @pl.when(first)
        def _():
            entry[...] = jnp.zeros_like(entry)

        for part in range(own):
            @pl.when(jnp.logical_not(first))
            def _():
                entry_copy(part).wait_recv()

            give_cores(part)
        for part in range(own):
            map_copy(part, 1).wait_send()

            @pl.when(jnp.logical_not(first))
            def _():
                map_copy(part, 0).wait_send()

    @pl.when((odd == 1) & first)
    def _():
        map_queries()
        for part in range(own):
            give_cores(part)

    @pl.when((odd == 1) & jnp.logical_not(first))
    def _():
        compose_chip()

        @pl.when(last)
        def _():
            map_queries()
            for part in range(own):
                pass_on(part)
                if part:
                    enter(part - 1)
            enter(own - 1)

        @pl.when(jnp.logical_not(last))
        def _():
            @pl.when(late)
            def _():
                map_queries()

            for part in range(own):
                pass_on(part)

            @pl.when(jnp.logical_not(late))
            def _():
                map_queries()

            for part in range(own):
                enter(part)

        for part in range(own):
            entry_copy(part).wait_send()

    @pl.when((odd == 1) & jnp.logical_not(last))
    def _():
        for part in range(own):
            chain_copy(part).wait_send()

    gain = gain_ref[...]
    for step in [0] + list(range(n_head - 1, 0, -1)):
        for part in range(own):
            if step:
                core_copy(n_head - step, part).wait_recv()
                core = core_in[step, part]
            else:
                core = core_out[part, me]
            core = core.astype(F32) + offset[step, part]
            scale = lax.rsqrt(jnp.mean(core * core, axis=-1, keepdims=True) + 1e-06)
            head = lax.rem(me + step, n_head) * own + part
            out_rows[pl.ds(head, tokens, stride=heads), :] = core * scale * gain
    out_ref[...] = out_rows[...].reshape(tokens, heads, width).astype(BF16)

    for step in range(1, n_head):
        terms_copy(step, 0).wait_send()
        terms_copy(step, 1).wait_send()
        solver_copy(step).wait_send()
        query_copy(step).wait_send()
        for part in range(own):
            core_copy(step, part).wait_send()


def solution(mesh):
    n_seq, n_head = mesh.shape["seq"], mesh.shape["head"]

    def local(queries, keys, values, log_decay, beta, norm_gain):
        tokens, heads, width = queries.shape
        own = heads // n_head
        length = tokens * heads
        hbm = pl.BlockSpec(memory_space=pltpu.HBM)
        payload = (n_head, 2 * own * tokens + 16, width)
        solvers = (n_head, max(own // 2, 1) * tokens, 2 * tokens)
        dma = pltpu.SemaphoreType.DMA
        return pl.pallas_call(
            functools.partial(kernel, n_seq, n_head),
            out_shape=pltpu.VMEM(queries.shape, BF16),
            in_specs=[hbm] * 6,
            out_specs=pl.BlockSpec(memory_space=pltpu.VMEM),
            scratch_shapes=[
                pltpu.VMEM(queries.shape, BF16),
                pltpu.VMEM(queries.shape, BF16),
                pltpu.VMEM(queries.shape, BF16),
                pltpu.VMEM((heads, tokens), BF16),
                pltpu.VMEM((heads, tokens), BF16),
                pltpu.VMEM((1, width), F32),
                pltpu.VMEM((length, width), F32),
                pltpu.VMEM((length, width), F32),
                pltpu.VMEM((length, width), F32),
                pltpu.VMEM((length, width), F32),
                pltpu.VMEM((heads, PACK * tokens), F32),
                pltpu.VMEM((heads, PACK * tokens), F32),
                pltpu.VMEM((2, heads, PACK * tokens), F32),
                pltpu.VMEM(payload, BF16),
                pltpu.VMEM(payload, BF16),
                pltpu.VMEM(solvers, BF16),
                pltpu.VMEM(solvers, BF16),
                pltpu.VMEM((n_head, own * tokens, width), BF16),
                pltpu.VMEM((n_head, own * tokens, width), BF16),
                pltpu.VMEM((n_head, own, tokens, width), F32),
                pltpu.VMEM((own, n_head, width, 2 * width), BF16),
                pltpu.VMEM((own, 3, width, width), BF16),
                pltpu.VMEM((own, width, width), F32),
                pltpu.VMEM((own, 3, width, width), BF16),
                pltpu.VMEM((own, 2, width, width), BF16),
                pltpu.VMEM((own, width, width), F32),
                pltpu.VMEM((own, width, width), BF16),
                pltpu.VMEM((own, n_head * tokens, width), BF16),
                pltpu.VMEM((own, n_head * tokens, width), F32),
                pltpu.VMEM((own, width, width), BF16),
                pltpu.VMEM((own, width, width), BF16),
                pltpu.VMEM((own, n_head, tokens, width), BF16),
                pltpu.VMEM((n_head, own, tokens, width), BF16),
                dma((6,)),
                dma((2, n_head)),
                dma((2, n_head)),
                dma((n_head,)),
                dma((n_head,)),
                dma((n_head,)),
                dma((n_head,)),
                dma((2, own)),
                dma((2, own)),
                dma((own,)),
                dma((own,)),
                dma((own,)),
                dma((own,)),
                dma((n_head, own)),
                dma((n_head, own)),
            ],
            compiler_params=pltpu.CompilerParams(
                collective_id=0, has_side_effects=True, vmem_limit_bytes=48 * 1024 * 1024
            ),
            name="gated_delta",
        )(*[
            pltpu.with_memory_space_constraint(array, pltpu.HBM)
            for array in (queries, keys, values, log_decay.T, beta.T, norm_gain.reshape(1, width))
        ])

    tokens_by_device = P(("seq", "head"), None, None)
    placed = (tokens_by_device,) * 3 + (P(("seq", "head"), None),) * 2 + (P(),)
    return jax.shard_map(
        local, mesh=mesh, in_specs=placed, out_specs=tokens_by_device, check_vma=False
    )
```
